256 devices in a mesh: section: 2 (over core), diam: 128 (over x, z, y).
Axes of the slice: x: 4, y: 4, z: 8, core: 2. Of those that a mesh axis runs over, the one named last changes fastest.
Arguments:
- modal: bfloat16 [2, 256, 19, 512, 128], P('section', 'diam'), may hold values from -6 to 6
- stiffness: bfloat16 [2, 256, 512, 512], P('section', 'diam'), may hold values from -0.25 to 0.25
- mass: bfloat16 [2, 256, 512, 512], P('section', 'diam'), may hold values from -0.25 to 0.25
- freq: float32 [128], replicated, may hold values from 0.02 to 0.11
- coupling: bfloat16 [2, 256, 4, 32, 32], P('section', 'diam'), may hold values from -1 to 1
- route: int32 [2, 19456, 1], P('section', 'diam'), may hold values from 0 to 127; in each aligned block of 152 rows (0 to 151, 152 to 303, ..., all dimensions but the last counted through in order) at most 2 rows name the same one
- target: int32 [2, 19456], P('section', 'diam'), may hold values from 0 to 151
- contact_dof: int32 [2, 16384], P('section', 'diam'), may hold values from 0 to 511
- evaluator: int32 [2, 16384, 1], P('section', 'diam'), may hold values from 0 to 127; in each aligned block of 128 rows (0 to 127, 128 to 255, ..., all dimensions but the last counted through in order) at most 2 rows name the same one
- preload: bfloat16 [2, 16384], P('section', 'diam'), may hold values from 0.5 to 13.5, as said below
Outputs:
- residual: bfloat16 [2, 256, 19, 512, 128], P('section', 'diam')
The draws below stay inside these ranges and needn't reach their ends.
Inputs may be any that keep to these rules, and one draw needn't show every extreme that they name: `route`: destination device of each tile on the other section; among the tiles of one device no destination appears more than 2 times, a bound that some block reaches; every destination appears. `evaluator`: joint of each row, one joint to each index of diam in the same section; among the rows of one device no joint appears more than 2 times, a bound that some block reaches; every joint has rows. `preload`: positive.
All inputs are finite; a program needn't handle non-finite values.
Results may differ from the reference program's by a relative error of at most 0.0028.
Values may be sent and summed in bfloat16 or wider, within the bound.
A program may use at most 128 MiB of HBM per device.

```python
import math
import jax
import jax.numpy as jnp
import numpy as np
from jax import lax

HARM = 9
NCOMP = 19
NDOF = 512
NIF = 128
NPATCH = 4
NIFP = 32
NT = 128
PTS = 128
ND_DEV = 2
CR_DEV = 128
NDG = 256
TILES_DEV = 152
CAP = 2
CROWS = 16384
CAPC = 2
N_DIAM = 128


def draw_preload(key, part):
    owner_device = (jnp.arange(CROWS) // CR_DEV).astype(jnp.float32)
    devices = CROWS // CR_DEV
    ramp = 1.0 + 2.0 * owner_device / max(devices - 1, 1)
    rough = jax.random.uniform(key, (2, CROWS), jnp.float32, 0.5, 1.5)
    values = rough * ramp[None, :]
    return values.astype(jnp.bfloat16)


def touch_ends(entries, stream_key, low, top_value):
    dims = entries.shape
    place = [jax.random.randint(jax.random.fold_in(stream_key, axis), (), 0, dims[axis]) for axis in range(len(dims))]
    entries = entries.at[tuple(place)].set(low)
    longest = dims.index(max(dims))
    place[longest] = (place[longest] + 1) % dims[longest]
    return entries.at[tuple(place)].set(top_value)


def shard_levels(rng, extent, split, low, largest):
    def one(dim, parts):
        steps = jax.random.uniform(jax.random.fold_in(jax.random.fold_in(rng, 6), dim), (parts,), jnp.float32, low / len(split), largest / len(split))
        return jnp.repeat(jnp.exp(steps), extent[dim] // parts).reshape((-1,) + (1,) * (len(extent) - dim - 1))

    gain = one(*split[0])
    for cut in split[1:]:
        gain = gain * one(*cut)
    return gain


def shared_out(key, own, number, rows, count, top, limit, slope):
    ranking = jax.random.permutation(key, count)
    packed, ordinary = shares(count, rows * top, limit, slope, True), shares(count, rows * top, limit, slope, False)
    places = jnp.arange(count)

    def named(sizes, offset_by):
        used = int((sizes > 0).sum())
        fixed = max(1, used // 4)
        moved = fixed + (places - fixed + offset_by * (used - fixed)) % max(1, count - fixed)
        return jnp.zeros((count,), jnp.int32).at[ranking[jnp.where(places < fixed, places, moved)]].set(jnp.asarray(sizes, jnp.int32))

    sizes = jnp.where(number % 4 == 0, named(packed, number // 4), named(ordinary, number - number // 4 - 1))
    mixed = jax.random.permutation(jax.random.fold_in(own, 3), count)
    giver, taker = mixed[0:count // 2 * 2:2], mixed[1:count // 2 * 2:2]
    room = jnp.minimum(sizes[giver] - 1, limit - sizes[taker]) // 2
    room = jnp.where((giver == ranking[0]) | (taker == ranking[0]) | (sizes[taker] == 0), 0, jnp.maximum(room, 0))
    moved = jax.random.randint(jax.random.fold_in(own, 4), (count // 2,), 0, 1 << 20) % (room + 1)
    sizes = sizes.at[giver].add(-moved).at[taker].add(moved)
    members = jnp.searchsorted(jnp.cumsum(sizes), jnp.arange(rows * top), side="right").astype(jnp.int32)
    table = members.reshape(top, rows).T
    table = table[jax.random.permutation(jax.random.fold_in(own, 1), rows)]
    offset_by = jax.random.randint(jax.random.fold_in(own, 2), (rows, 1), 0, top)
    return jnp.take_along_axis(table, (jnp.arange(top)[None, :] + offset_by) % top, axis=1)


def shares(number_of, total, bound, skew, full):
    portions = [(1 << 20) // math.isqrt(rank ** skew) + 1 for rank in range(1, number_of + 1)]
    largest = bound if full else min(bound, max(-(-total // number_of), total * portions[0] // sum(portions)))
    least = 1 if total - largest >= number_of - 1 else 0
    holding, spare = [largest] + [least] * (number_of - 1), total - largest - least * (number_of - 1)
    while spare > 0:
        candidates = [i for i in range(1, number_of) if holding[i] < largest] or [i for i in range(1, number_of) if holding[i] < bound]
        whole, budget = sum([portions[i] for i in candidates]), spare
        for i in candidates:
            more = min(bound - holding[i], max(1, budget * portions[i] // whole), spare)
            holding[i] = holding[i] + more
            spare = spare - more
    return np.array(holding)


def noise(stream_key, dims, scale, most, split=(), held_as=jnp.bfloat16):
    result = scale * jax.random.normal(stream_key, dims, jnp.float32)
    if split:
        result = result * shard_levels(stream_key, dims, split, -0.22, 0.18)
    return jnp.clip(result, -most, most).astype(held_as)


def setup_inputs(seed: int = 0) -> dict:
    key_list = jax.random.split(jax.random.key(seed), 11)
    modal = noise(key_list[0], (2, NDG, NCOMP, NDOF, PTS), 1.0, 6.0, ((0, 2), (1, 128)))
    stiffness = noise(key_list[1], (2, NDG, NDOF, NDOF), NDOF ** -0.5, 0.25, ((0, 2), (1, 128)))
    mass = noise(key_list[2], (2, NDG, NDOF, NDOF), NDOF ** -0.5, 0.25, ((0, 2), (1, 128)))
    freq = jnp.clip(jnp.exp(jax.random.uniform(key_list[3], (PTS,), jnp.float32, math.log(0.02), math.log(0.11))), 0.02, 0.11)
    coupling = noise(key_list[4], (2, NDG, NPATCH, NIFP, NIFP), NIFP ** -0.5, 1.0, ((0, 2), (1, 128)))
    route_keys = jax.random.split(jax.random.fold_in(key_list[5], 1), 2 * (NDG * NCOMP * NPATCH) // TILES_DEV)
    route_turns = jax.random.permutation(jax.random.fold_in(key_list[5], 3), 2 * (NDG * NCOMP * NPATCH) // TILES_DEV)
    route = jax.vmap(lambda own, number: shared_out(jax.random.fold_in(key_list[5], 2), own, number, TILES_DEV, N_DIAM, 1, CAP, 1))(route_keys, route_turns).reshape((2, NDG * NCOMP * NPATCH, 1))
    target = touch_ends(jax.random.randint(key_list[6], (2, NDG * NCOMP * NPATCH), 0, TILES_DEV), jax.random.fold_in(key_list[6], 1), 0, TILES_DEV - 1).astype(jnp.int32)
    contact_dof = touch_ends(jax.random.randint(key_list[7], (2, CROWS), 0, ND_DEV * NDOF // 2), jax.random.fold_in(key_list[7], 1), 0, (ND_DEV * NDOF // 2) - 1).astype(jnp.int32)
    evaluator_keys = jax.random.split(jax.random.fold_in(key_list[8], 1), 2 * CROWS // CR_DEV)
    evaluator_turns = jax.random.permutation(jax.random.fold_in(key_list[8], 3), 2 * CROWS // CR_DEV)
    evaluator = jax.vmap(lambda own, number: shared_out(jax.random.fold_in(key_list[8], 2), own, number, CR_DEV, N_DIAM, 1, CAPC, 2))(evaluator_keys, evaluator_turns).reshape((2, CROWS, 1))
    preload = draw_preload(jax.random.fold_in(key_list[10], 71), 0)
    return {"modal": modal, "stiffness": stiffness, "mass": mass, "freq": freq, "coupling": coupling, "route": route, "target": target, "contact_dof": contact_dof, "evaluator": evaluator, "preload": preload}


JOINT_STIFFNESS = 0.3
FRICTION = 0.6
SMOOTHING = 0.1

def harmonic_order():
    comp_index = jnp.arange(NCOMP)
    return jnp.where(comp_index <= HARM, comp_index, comp_index - HARM).astype(jnp.float32)

def time_tables():
    comp_index = jnp.arange(NCOMP)
    harm_order = harmonic_order()
    tau_grid = jnp.arange(NT).astype(jnp.float32) * (2.0 * math.pi / NT)
    phase = harm_order[:, None] * tau_grid[None, :]
    is_sine = (comp_index > HARM)[:, None]
    slope_table = jnp.where(is_sine, harm_order[:, None] * jnp.cos(phase), -harm_order[:, None] * jnp.sin(phase))
    shape_table = jnp.where(is_sine, jnp.sin(phase), jnp.cos(phase))
    weights = jnp.where(comp_index == 0, 1.0 / NT, 2.0 / NT).astype(jnp.float32)
    projection = jnp.transpose(shape_table * weights[:, None])
    return (slope_table.astype(jnp.float32), projection.astype(jnp.float32))

def joint_forces(payload, pressure, joint_mean, freq, slope_table, projection):
    coefficient = payload.astype(jnp.float32)
    velocity = freq[None, None, :, None] * jnp.einsum('scjp,ct->sjpt', coefficient, slope_table, precision=lax.Precision.HIGHEST)
    slip_speed = jnp.sqrt(velocity[:, 0] ** 2 + velocity[:, 1] ** 2 + SMOOTHING ** 2)
    sliding = FRICTION * pressure[:, None, None, None] * velocity / slip_speed[:, None]
    harmonic = jnp.einsum('sjpt,tc->scjp', sliding, projection, precision=lax.Precision.HIGHEST)
    return (JOINT_STIFFNESS * (coefficient - joint_mean) + harmonic).astype(jnp.bfloat16)

def reference(modal, stiffness, mass, freq, coupling, route, target, contact_dof, evaluator, preload):
    slope_table, projection = time_tables()
    omega_square = (harmonic_order()[:, None] * freq[None, :]) ** 2
    half_dof = NDOF // 2
    tiles_dev = ND_DEV * NCOMP * NPATCH
    tile_count = N_DIAM * tiles_dev
    section_results = []
    for which_section in range(2):
        other_section = 1 - which_section
        send_tiles = modal[other_section][:, :, :NIF, :].astype(jnp.float32).reshape(tile_count, NIFP, PTS)
        segment_ids = route[other_section, :, 0] * tiles_dev + target[other_section]
        glued = jax.ops.segment_sum(send_tiles, segment_ids, num_segments=tile_count).astype(jnp.bfloat16)
        glued = glued.reshape(N_DIAM, ND_DEV, NCOMP, NPATCH, NIFP, PTS)
        preloads = preload[which_section].astype(jnp.float32)
        joint_index = evaluator[which_section, :, 0]
        owner_device = jnp.arange(CROWS) // CR_DEV
        block_index = owner_device * ND_DEV + contact_dof[which_section] // half_dof
        dof_pair = contact_dof[which_section] % half_dof
        by_pairs = modal[which_section].reshape(NDG, NCOMP, half_dof, 2, PTS)
        payload = by_pairs[block_index[:, None], jnp.arange(NCOMP)[None, :], dof_pair[:, None]]
        joint_load = jax.ops.segment_sum(preloads, joint_index, num_segments=N_DIAM)
        weighted = jax.ops.segment_sum(preloads[:, None, None, None] * payload.astype(jnp.float32), joint_index, num_segments=N_DIAM)
        joint_mean = weighted / joint_load[:, None, None, None]
        pressure = preloads * CR_DEV / joint_load[joint_index]

        def on_rows(packed_args):
            part_payload, part_pressure, part_joint = packed_args
            return joint_forces(part_payload, part_pressure, joint_mean[part_joint], freq, slope_table, projection)
        contact_force = lax.map(on_rows, (payload.reshape(N_DIAM, CR_DEV, NCOMP, 2, PTS), pressure.reshape(N_DIAM, CR_DEV), joint_index.reshape(N_DIAM, CR_DEV)))

        def on_device(packed_args):
            field, stiff_w, mass_w, glued_tile, coupling_tile, force_rows, dof_list = packed_args
            field_wide = field.astype(jnp.float32)
            stiff_part = jnp.einsum('bcdp,bde->bcep', field_wide, stiff_w.astype(jnp.float32))
            inertia = jnp.einsum('bcdp,bde->bcep', field_wide, mass_w.astype(jnp.float32))
            residual = stiff_part - omega_square[None, :, None, :] * inertia
            linkage = jnp.einsum('bcqip,bqij->bcqjp', glued_tile.astype(jnp.float32), coupling_tile.astype(jnp.float32))
            residual = residual.at[:, :, :NIF, :].add(linkage.reshape(ND_DEV, NCOMP, NIF, PTS))
            split_rows = residual.reshape(ND_DEV, NCOMP, half_dof, 2, PTS)
            split_rows = split_rows.at[(dof_list // half_dof)[:, None], jnp.arange(NCOMP)[None, :], (dof_list % half_dof)[:, None]].add(force_rows.astype(jnp.float32))
            return split_rows.reshape(ND_DEV, NCOMP, NDOF, PTS).astype(jnp.bfloat16)
        device_out = lax.map(on_device, (modal[which_section].reshape(N_DIAM, ND_DEV, NCOMP, NDOF, PTS), stiffness[which_section].reshape(N_DIAM, ND_DEV, NDOF, NDOF), mass[which_section].reshape(N_DIAM, ND_DEV, NDOF, NDOF), glued, coupling[which_section].reshape(N_DIAM, ND_DEV, NPATCH, NIFP, NIFP), contact_force, contact_dof[which_section].reshape(N_DIAM, CR_DEV)))
        section_results.append(device_out.reshape(NDG, NCOMP, NDOF, PTS))
    return jnp.stack(section_results)
```

```python
import functools
import math

import jax
import jax.numpy as jnp
import ml_dtypes
import numpy as np
from jax import lax
from jax.experimental import pallas as pl
from jax.experimental.pallas import tpu as pltpu
from jax.sharding import PartitionSpec as P

HARM = 9
NC = 19
ND = 512
NIF = 128
NT = 128
PTS = 128
NX, NZ, NY = 4, 8, 4
NDEV = 128
TILES = 152
ROWS = 128
STIFF = 0.3
FRICTION = 0.6
MESH = pl.DeviceIdType.MESH
BF = jnp.bfloat16
F32 = jnp.float32


def high_low(table):
    high = table.astype(ml_dtypes.bfloat16)
    low = (table - high.astype(np.float64)).astype(ml_dtypes.bfloat16)
    return high, low


def fourier_tables():
    comp = np.arange(NC)
    order = np.where(comp <= HARM, comp, comp - HARM).astype(np.float64)
    phase = order[:, None] * (np.arange(NT) * (2.0 * math.pi / NT))[None, :]
    sine = (comp > HARM)[:, None]
    slope = np.where(sine, order[:, None] * np.cos(phase), -order[:, None] * np.sin(phase))
    shape = np.where(sine, np.sin(phase), np.cos(phase))
    weight = np.where(comp == 0, 1.0 / NT, 2.0 / NT)
    eye = np.eye(8)
    s_hi, s_lo = high_low(slope[1:].T)
    p_hi, p_lo = high_low(shape * weight[:, None])
    spread = lambda t: np.kron(t.astype(np.float64), eye).astype(ml_dtypes.bfloat16)
    slope_table = np.concatenate([spread(s_hi), spread(s_lo)], axis=1)
    proj_table = np.concatenate([spread(p_hi), spread(p_lo)], axis=0)
    return slope_table, proj_table


def dot(a, b):
    return jnp.dot(a, b, preferred_element_type=F32)


def main_kernel(
    src_ref, modal, stiff, mass, freq, rows_ref, tags, slope_t, proj_t,
    part_f, part_b, got, got_tags,
    packed, psend, rx, ysend, ry, zsend, rz, agz, agy, agx,
    pay, harm, force, resid, stm, scat,
    s_send, s_recv, t_send, t_recv, r_send, r_recv,
):
    sec = lax.axis_index("section")
    me = lax.axis_index("diam")
    other = 1 - sec
    x = me // (NZ * NY)
    z = lax.rem(me // NY, NZ)
    y = lax.rem(me, NY)

    def at(px, pz, py):
        return (px * NZ + pz) * NY + py

    def x_peer(k):
        return lax.rem(x + k, NX)

    def y_peer(k):
        return lax.rem(y + k, NY)

    def z_peer(k):
        return lax.rem(z + k, NZ)

    barrier = pltpu.get_barrier_semaphore()

    def hail(k, carry):
        pl.semaphore_signal(barrier, inc=1, device_id=(other, k), device_id_type=MESH)
        return carry

    lax.fori_loop(0, NDEV, hail, 0)
    for k in range(1, NX):
        pl.semaphore_signal(barrier, inc=1, device_id=(sec, at(x_peer(k), z, y)), device_id_type=MESH)
    for k in range(1, NY):
        pl.semaphore_signal(barrier, inc=1, device_id=(sec, at(x, z, y_peer(k))), device_id_type=MESH)
    for k in range(1, NZ):
        pl.semaphore_signal(barrier, inc=1, device_id=(sec, at(x, z_peer(k), y)), device_id_type=MESH)

    def pack(d, carry):
        packed[d, 0:32, :] = modal[src_ref[2 * d]]
        packed[d, 32:64, :] = modal[src_ref[2 * d + 1]]
        return carry

    lax.fori_loop(0, NDEV, pack, 0)
    pl.semaphore_wait(barrier, NDEV + NX + NY + NZ - 3)

    def send_tiles(first, count):
        def one(k, carry):
            px = lax.rem(x + k // (NZ * NY), NX)
            pz = lax.rem(z + lax.rem(k // NY, NZ), NZ)
            py = lax.rem(y + lax.rem(k, NY), NY)
            d = at(px, pz, py)
            pltpu.make_async_remote_copy(
                src_ref=tags.at[d], dst_ref=got_tags.at[me], send_sem=t_send, recv_sem=t_recv,
                device_id=(other, d), device_id_type=MESH,
            ).start()
            pltpu.make_async_remote_copy(
                src_ref=packed.at[d], dst_ref=got.at[me], send_sem=s_send, recv_sem=s_recv,
                device_id=(other, d), device_id_type=MESH,
            ).start()
            return carry

        lax.fori_loop(first, first + count, one, 0)

    send_tiles(0, 32)

    pre_row = rows_ref[0:1, :]
    eval_row = rows_ref[1:2, :]
    dof_row = rows_ref[2:3, :]
    dof_col = jnp.transpose(jnp.broadcast_to(dof_row, (ROWS, ROWS)))
    lane512 = lax.broadcasted_iota(jnp.int32, (ROWS, ND), 1).astype(F32)
    sub512 = lax.broadcasted_iota(jnp.int32, (ND, ROWS), 0).astype(F32)
    picks = []
    for g in range(2):
        halves = []
        for a in range(2):
            here = dof_col[:, 0:1] * 2.0 + (a - g * ND)
            halves.append(jnp.where(lane512 == here, 1.0, 0.0).astype(BF))
            there = dof_row * 2.0 + (a - g * ND)
            scat[g, :, a * ROWS:(a + 1) * ROWS] = jnp.where(sub512 == there, 1.0, 0.0).astype(BF)
        picks.append(jnp.concatenate(halves, axis=0))
    sub128 = lax.broadcasted_iota(jnp.int32, (ROWS, ROWS), 0).astype(F32)
    weights32 = jnp.where(sub128 == eval_row, pre_row, 0.0)
    weights = weights32.astype(BF)
    load = jnp.broadcast_to(jnp.sum(weights32, axis=1, keepdims=True), (NDEV, PTS))
    load_hi = load.astype(BF)
    psend[:, :, 38] = load_hi.reshape(NX, 2, 16, PTS)
    psend[:, :, 39] = (load - load_hi.astype(F32)).astype(BF).reshape(NX, 2, 16, PTS)

    def comps(g, c, n):
        tiles = [modal[pl.ds(((g * NC) + c + i) * 16, 16)].reshape(ND, PTS) for i in range(n)]
        return tiles[0] if n == 1 else jnp.concatenate(tiles, axis=1)

    def gather(c, n):
        got_rows = dot(picks[0], comps(0, c, n)) + dot(picks[1], comps(1, c, n))
        narrow = got_rows.astype(BF)
        for i in range(n):
            pay[c + i] = got_rows[:, i * PTS:(i + 1) * PTS]
        for a in range(2):
            summed = dot(weights, narrow[a * ROWS:(a + 1) * ROWS]).astype(BF)
            for i in range(n):
                psend[:, :, (c + i) * 2 + a] = summed[:, i * PTS:(i + 1) * PTS].reshape(NX, 2, 16, PTS)

    def gather_pair(i, carry):
        gather(2 * i, 2)
        return carry

    lax.fori_loop(0, 9, gather_pair, 0)
    gather(18, 1)

    def push(src, dst, step, device):
        pltpu.make_async_remote_copy(
            src_ref=src, dst_ref=dst, send_sem=r_send.at[step], recv_sem=r_recv.at[step],
            device_id=device, device_id_type=MESH,
        ).start()

    def arrived(ref, step):
        pltpu.make_async_copy(ref, ref, r_recv.at[step]).wait()

    def left(ref, step):
        pltpu.make_async_copy(ref, ref, r_send.at[step]).wait()

    for k in range(1, NX):
        push(psend.at[x_peer(k)], rx.at[x], 0, (sec, at(x_peer(k), z, y)))
    send_tiles(32, 32)

    for g in range(2):
        stm[g, 0:ND] = jnp.transpose(stiff[g])
        stm[g, ND:2 * ND] = jnp.transpose(mass[g])

    soft = 0.01 / (freq[...] * freq[...])

    def contact(b, carry):
        low = pl.multiple_of(b * 8, 8)
        sides = []
        for a in range(2):
            lines = [pay[c, pl.ds(a * ROWS + low, 8), :] for c in range(1, NC)]
            sides.append(jnp.concatenate(lines, axis=0))
        values = jnp.concatenate(sides, axis=1).astype(BF)
        speed = dot(slope_t[...], jnp.concatenate([values, values], axis=0))
        one, two = speed[:, 0:PTS], speed[:, PTS:2 * PTS]
        inverse = lax.rsqrt(one * one + two * two + soft)
        slide = jnp.concatenate([(one * inverse).astype(BF), (two * inverse).astype(BF)], axis=1)
        both = dot(proj_t[...], slide)
        total = both[0:8 * NC] + both[8 * NC:16 * NC]
        for c in range(NC):
            for a in range(2):
                harm[c, pl.ds(a * ROWS + low, 8), :] = total[8 * c:8 * c + 8, a * PTS:(a + 1) * PTS]
        return carry

    lax.fori_loop(0, 8, contact, 0)

    arrived(rx.at[0:3], 0)
    whole = psend[x].astype(F32)
    for k in range(1, NX):
        whole = whole + rx[x_peer(k)].astype(F32)
    total = whole[:, 38] + whole[:, 39]
    total_hi = total.astype(BF)
    for g in range(2):
        for part in range(2):
            ysend[2 * g + part] = whole[g, 20 * part:20 * part + 20].astype(BF)
        ysend[2 * g + 1, 18] = total_hi[g]
        ysend[2 * g + 1, 19] = (total[g] - total_hi[g].astype(F32)).astype(BF)
    for k in range(1, NY):
        push(ysend.at[y_peer(k)], ry.at[y], 1, (sec, at(x, z, y_peer(k))))
    send_tiles(64, 32)
    lax.fori_loop(8, 16, contact, 0)

    arrived(ry.at[0:3], 1)
    whole = ysend[y].astype(F32)
    for k in range(1, NY):
        whole = whole + ry[y_peer(k)].astype(F32)
    total = whole[18] + whole[19]
    total_hi = total.astype(BF)
    odd = lax.rem(y, 2) == 1
    zsend[0:18] = whole[0:18].astype(BF)
    zsend[18] = jnp.where(odd, total, whole[18]).astype(BF)
    zsend[19] = jnp.where(odd, total - total_hi.astype(F32), whole[19]).astype(BF)
    zsend[20:24] = jnp.zeros((4, 16, PTS), BF)
    for k in range(1, NZ):
        push(zsend.at[pl.ds(3 * z_peer(k), 3)], rz.at[z], 2, (sec, at(x, z_peer(k), y)))
    send_tiles(96, 32)

    def balance(g, c, n):
        both = dot(stm[g], comps(g, c, n))
        for i in range(n):
            h = jnp.where(c + i <= HARM, c + i, c + i - HARM)
            scaled = jnp.asarray(h, jnp.int32).astype(F32) * freq[...]
            lanes = slice(i * PTS, (i + 1) * PTS)
            resid[g * NC + c + i] = both[0:ND, lanes] - (scaled * scaled) * both[ND:2 * ND, lanes]

    def balance_pair(g, i, carry):
        balance(g, 2 * i, 2)
        return carry

    lax.fori_loop(0, 9, functools.partial(balance_pair, 0), 0)
    balance(0, 18, 1)

    arrived(rz.at[0:7], 2)
    whole = zsend[pl.ds(3 * z, 3)].astype(F32)
    for k in range(1, NZ):
        whole = whole + rz[z_peer(k)].astype(F32)
    total = whole[0] + whole[1]
    total_hi = total.astype(BF)
    loads = jnp.logical_and(odd, z == 6)
    agz[3 * z] = jnp.where(loads, total, whole[0]).astype(BF)
    agz[3 * z + 1] = jnp.where(loads, total - total_hi.astype(F32), whole[1]).astype(BF)
    agz[3 * z + 2] = whole[2].astype(BF)
    for k in range(1, NZ):
        mine = agz.at[pl.ds(3 * z, 3)]
        push(mine, mine, 3, (sec, at(x, z_peer(k), y)))
    lax.fori_loop(0, 4, functools.partial(balance_pair, 1), 0)
    arrived(agz.at[0:21], 3)
    agy[pl.ds(20 * y, 20)] = agz[0:20]
    for k in range(1, NY):
        push(agz.at[0:20], agy.at[pl.ds(20 * y, 20)], 4, (sec, at(x, z, y_peer(k))))
    lax.fori_loop(4, 6, functools.partial(balance_pair, 1), 0)
    arrived(agy.at[0:60], 4)
    agx[x] = agy[...].reshape(2, 40, 16, PTS)
    for k in range(1, NX):
        push(agx.at[x], agx.at[x], 5, (sec, at(x_peer(k), z, y)))
    lax.fori_loop(6, 9, functools.partial(balance_pair, 1), 0)
    balance(1, 18, 1)
    arrived(agx.at[0:3], 5)

    lane128 = lax.broadcasted_iota(jnp.int32, (ROWS, ROWS), 1).astype(F32)
    eval_col = jnp.transpose(jnp.broadcast_to(eval_row, (ROWS, ROWS)))
    pre_col = jnp.transpose(jnp.broadcast_to(pre_row, (ROWS, ROWS)))
    choose = jnp.where(lane128 == eval_col, 1.0, 0.0).astype(BF)

    def joints(k):
        return agx[:, :, k].reshape(NDEV, PTS)

    loaded = dot(choose, jnp.concatenate([joints(38), joints(39)], axis=1))
    per_load = 1.0 / (loaded[:, 0:PTS] + loaded[:, PTS:2 * PTS])
    pressed = pre_col * (FRICTION * ROWS) * per_load

    def forces(c, carry):
        mean = dot(choose, jnp.concatenate([joints(2 * c), joints(2 * c + 1)], axis=1))
        for a in range(2):
            rows = slice(a * ROWS, (a + 1) * ROWS)
            away = pay[c, rows, :] - mean[:, a * PTS:(a + 1) * PTS] * per_load
            force[c, rows, :] = (STIFF * away + pressed * harm[c, rows, :]).astype(BF)
        return carry

    lax.fori_loop(0, NC, forces, 0)

    def finish(g, c, n):
        lines = [force[c + i] for i in range(n)]
        added = dot(scat[g], lines[0] if n == 1 else jnp.concatenate(lines, axis=1))
        for i in range(n):
            item = g * NC + c + i
            value = resid[item] + added[:, i * PTS:(i + 1) * PTS]
            part_f[item] = value[0:NIF]
            part_b[item] = value[NIF:ND].astype(BF)

    def finish_pair(g, i, carry):
        finish(g, 2 * i, 2)
        return carry

    for g in range(2):
        lax.fori_loop(0, 9, functools.partial(finish_pair, g), 0)
        finish(g, 18, 1)

    left(rx.at[0:3], 0)
    left(ry.at[0:3], 1)
    left(rz.at[0:7], 2)
    left(rz.at[0:7], 3)
    left(agy.at[0:60], 4)
    left(agx.at[0:3], 5)
    pltpu.make_async_copy(packed, packed, s_send).wait()
    pltpu.make_async_copy(tags, tags, t_send).wait()
    pltpu.make_async_copy(got_tags, got_tags, t_recv).wait()
    pltpu.make_async_copy(got, got, s_recv).wait()


def last_kernel(tag_ref, got, part_f, part_b, link, out, glued):
    step = pl.program_id(0)

    @pl.when(step == 0)
    def _():
        glued[...] = jnp.zeros_like(glued)

        def add(d, carry):
            for s in range(2):
                slot = tag_ref[2 * d + s]
                glued[slot] = glued[slot] + got[d, 32 * s:32 * s + 32, :].astype(F32)
            return carry

        lax.fori_loop(0, NDEV, add, 0)

    for i in range(2):
        item = step * 2 + i
        tiles = glued[pl.ds(item * 4, 4)].reshape(NIF, PTS).astype(BF)
        out[i, 0:NIF, :] = (part_f[i] + dot(link[item // NC], tiles)).astype(BF)
        out[i, NIF:ND, :] = part_b[i]


def body(modal, stiffness, mass, freq, coupling, route, target, contact_dof, evaluator, preload):
    tiles = modal.reshape(2 * NC * 16, 32, PTS)
    place = jnp.arange(TILES, dtype=jnp.int32)
    key = (place * 256 + target[0])[None, :]
    named = route[0, :, 0][None, :] == jnp.arange(NDEV, dtype=jnp.int32)[:, None]
    first = jnp.min(jnp.where(named, key, 1 << 20), axis=1)
    final = jnp.max(jnp.where(named, key, -1), axis=1)
    pair = jnp.stack([jnp.where(first < (1 << 20), first, TILES),
                      jnp.where((final >= 0) & (final != first), final, TILES)], axis=1)
    spot = pair // 256
    src = ((spot // 4) * 16 + spot % 4).reshape(2 * NDEV)
    tags = jnp.broadcast_to((pair % 256)[:, :, None], (NDEV, 2, 64)).reshape(NDEV, 1, 128)
    rows = jnp.concatenate([
        preload.astype(F32), evaluator[:, :, 0].astype(F32), contact_dof.astype(F32),
        jnp.zeros((5, ROWS), F32)], axis=0)
    same = jnp.eye(4, dtype=jnp.bool_)[None, :, None, :, None]
    link = jnp.where(same, jnp.swapaxes(coupling[0], 2, 3)[:, :, :, None, :], 0).astype(BF)
    link = link.reshape(2, NIF, NIF)
    slope_table, proj_table = fourier_tables()

    vmem = pl.BlockSpec(memory_space=pltpu.VMEM)
    anywhere = pl.BlockSpec(memory_space=pl.ANY)
    dma = pltpu.SemaphoreType.DMA
    part_f, part_b, got, got_tags = pl.pallas_call(
        main_kernel,
        out_shape=(
            jax.ShapeDtypeStruct((2 * NC, NIF, PTS), F32),
            jax.ShapeDtypeStruct((2 * NC, ND - NIF, PTS), BF),
            jax.ShapeDtypeStruct((NDEV, 64, PTS), BF),
            jax.ShapeDtypeStruct((NDEV, 1, 128), jnp.int32),
        ),
        in_specs=[pl.BlockSpec(memory_space=pltpu.SMEM)] + [vmem] * 8,
        out_specs=(vmem, vmem, anywhere, anywhere),
        scratch_shapes=[
            pltpu.VMEM((NDEV, 64, PTS), BF),
            pltpu.VMEM((NX, 2, 40, 16, PTS), BF),
            pltpu.VMEM((NX, 2, 40, 16, PTS), BF),
            pltpu.VMEM((NY, 20, 16, PTS), BF),
            pltpu.VMEM((NY, 20, 16, PTS), BF),
            pltpu.VMEM((24, 16, PTS), BF),
            pltpu.VMEM((NZ, 3, 16, PTS), BF),
            pltpu.VMEM((24, 16, PTS), BF),
            pltpu.VMEM((80, 16, PTS), BF),
            pltpu.VMEM((NX, 2, 40, 16, PTS), BF),
            pltpu.VMEM((NC, 2 * ROWS, PTS), F32),
            pltpu.VMEM((NC, 2 * ROWS, PTS), F32),
            pltpu.VMEM((NC, 2 * ROWS, PTS), BF),
            pltpu.VMEM((2 * NC, ND, PTS), F32),
            pltpu.VMEM((2, 2 * ND, ND), BF),
            pltpu.VMEM((2, ND, 2 * ROWS), BF),
            dma, dma, dma, dma, dma((6,)), dma((6,)),
        ],
        compiler_params=pltpu.CompilerParams(
            collective_id=1, has_side_effects=True, vmem_limit_bytes=58 << 20
        ),
    )(src, tiles, stiffness[0], mass[0], freq.reshape(1, PTS), rows, tags,
      jnp.asarray(slope_table), jnp.asarray(proj_table))

    tag_list = jnp.concatenate([got_tags[:, :, 0], got_tags[:, :, 64]], axis=1).reshape(2 * NDEV)
    out = pl.pallas_call(
        last_kernel,
        grid=(NC,),
        out_shape=jax.ShapeDtypeStruct((2 * NC, ND, PTS), BF),
        in_specs=[
            pl.BlockSpec(memory_space=pltpu.SMEM),
            pl.BlockSpec((NDEV, 64, PTS), lambda i: (0, 0, 0)),
            pl.BlockSpec((2, NIF, PTS), lambda i: (i, 0, 0)),
            pl.BlockSpec((2, ND - NIF, PTS), lambda i: (i, 0, 0)),
            pl.BlockSpec((2, NIF, NIF), lambda i: (0, 0, 0)),
        ],
        out_specs=pl.BlockSpec((2, ND, PTS), lambda i: (i, 0, 0)),
        scratch_shapes=[pltpu.VMEM((TILES + 1, 32, PTS), F32)],
        compiler_params=pltpu.CompilerParams(vmem_limit_bytes=32 << 20),
    )(tag_list, got, part_f, part_b, link)
    return out.reshape(1, 2, NC, ND, PTS)


def solution(mesh):
    placed = (
        P("section", "diam", None, None, None),
        P("section", "diam", None, None),
        P("section", "diam", None, None),
        P(),
        P("section", "diam", None, None, None),
        P("section", "diam", None),
        P("section", "diam"),
        P("section", "diam"),
        P("section", "diam", None),
        P("section", "diam"),
    )
    return jax.shard_map(
        body,
        mesh=mesh,
        in_specs=placed,
        out_specs=P("section", "diam", None, None, None),
        check_vma=False,
    )
```

```python
import functools
import math

import jax
import jax.numpy as jnp
import ml_dtypes
import numpy as np
from jax import lax
from jax.experimental import pallas as pl
from jax.experimental.pallas import tpu as pltpu
from jax.sharding import PartitionSpec as P

HARM = 9
NC = 19
ND = 512
NIF = 128
NT = 128
PTS = 128
NX, NZ, NY = 4, 8, 4
NDEV = 128
TILES = 152
ROWS = 128
STIFF = 0.3
FRICTION = 0.6
MESH = pl.DeviceIdType.MESH
BF = jnp.bfloat16
F32 = jnp.float32


def high_low(table):
    high = table.astype(ml_dtypes.bfloat16)
    low = (table - high.astype(np.float64)).astype(ml_dtypes.bfloat16)
    return high, low


def fourier_tables():
    comp = np.arange(NC)
    order = np.where(comp <= HARM, comp, comp - HARM).astype(np.float64)
    phase = order[:, None] * (np.arange(NT) * (2.0 * math.pi / NT))[None, :]
    sine = (comp > HARM)[:, None]
    slope = np.where(sine, order[:, None] * np.cos(phase), -order[:, None] * np.sin(phase))
    shape = np.where(sine, np.sin(phase), np.cos(phase))
    weight = np.where(comp == 0, 1.0 / NT, 2.0 / NT)
    eye = np.eye(8)
    s_hi, s_lo = high_low(slope[1:].T)
    p_hi, p_lo = high_low(shape * weight[:, None])
    spread = lambda t: np.kron(t.astype(np.float64), eye).astype(ml_dtypes.bfloat16)
    slope_table = np.concatenate([spread(s_hi), spread(s_lo)], axis=1)
    proj_table = np.concatenate([spread(p_hi), spread(p_lo)], axis=0)
    return slope_table, proj_table


def dot(a, b):
    return jnp.dot(a, b, preferred_element_type=F32)


def main_kernel(
    modal_h, stiff_h, mass_h, freq, pre_ref, eval_ref, dof_ref, route_ref, target_ref,
    slope_t, proj_t,
    part_f, part_b, got, got_tags,
    edge, inner, stiff, mass, source, source_s, tags, packed,
    psend, rx, ysend, ry, zsend, rz, agz, agy, agx,
    pay, harm, force, resid, stm, scat, near, far,
    l_sem, s_send, s_recv, t_send, t_recv, r_send, r_recv,
):
    sec = lax.axis_index("section")
    me = lax.axis_index("diam")
    other = 1 - sec
    x = me // (NZ * NY)
    z = lax.rem(me // NY, NZ)
    y = lax.rem(me, NY)

    def at(px, pz, py):
        return (px * NZ + pz) * NY + py

    def x_peer(k):
        return lax.rem(x + k, NX)

    def y_peer(k):
        return lax.rem(y + k, NY)

    def z_peer(k):
        return lax.rem(z + k, NZ)

    loads = [
        pltpu.make_async_copy(modal_h.at[:, 0:4], edge, l_sem.at[0]),
        pltpu.make_async_copy(modal_h.at[:, 4:16], inner, l_sem.at[1]),
        pltpu.make_async_copy(stiff_h, stiff, l_sem.at[2]),
        pltpu.make_async_copy(mass_h, mass, l_sem.at[3]),
    ]
    for load in loads:
        load.start()

    barrier = pltpu.get_barrier_semaphore()

    def hail(k, carry):
        pl.semaphore_signal(barrier, inc=1, device_id=(other, k), device_id_type=MESH)
        return carry

    lax.fori_loop(0, NDEV, hail, 0)
    for k in range(1, NX):
        pl.semaphore_signal(barrier, inc=1, device_id=(sec, at(x_peer(k), z, y)), device_id_type=MESH)
    for k in range(1, NY):
        pl.semaphore_signal(barrier, inc=1, device_id=(sec, at(x, z, y_peer(k))), device_id_type=MESH)
    for k in range(1, NZ):
        pl.semaphore_signal(barrier, inc=1, device_id=(sec, at(x, z_peer(k), y)), device_id_type=MESH)

    spot = lax.broadcasted_iota(jnp.int32, (NDEV, TILES), 1)
    named = route_ref[...] == lax.broadcasted_iota(jnp.int32, (NDEV, TILES), 0)
    key = (spot * 256 + target_ref[...])
    first = jnp.min(jnp.where(named, key, 1 << 20), axis=1, keepdims=True)
    final = jnp.max(jnp.where(named, key, -1), axis=1, keepdims=True)
    none = jnp.full_like(first, TILES)
    one_key = jnp.where(first < (1 << 20), first, none)
    two_key = jnp.where((final >= 0) & (final != first), final, none)
    lane = lax.broadcasted_iota(jnp.int32, (NDEV, 128), 1)
    keys = jnp.where(lane < 64, one_key, two_key)
    source[...] = jnp.right_shift(keys, 8)
    tags[...] = jnp.bitwise_and(keys, 255).reshape(NDEV, 1, 128)
    listing = pltpu.make_async_copy(source, source_s, l_sem.at[4])
    listing.start()
    listing.wait()
    loads[0].wait()

    def tile(t):
        return edge[jnp.right_shift(t, 2), jnp.bitwise_and(t, 3)]

    def pack(d, carry):
        packed[d, 0:32, :] = tile(source_s[d, 0])
        packed[d, 32:64, :] = tile(source_s[d, 64])
        return carry

    lax.fori_loop(0, NDEV, pack, 0)
    pl.semaphore_wait(barrier, NDEV + NX + NY + NZ - 3)

    def send_one(k):
        px = lax.rem(x + k // (NZ * NY), NX)
        pz = lax.rem(z + lax.rem(k, NZ), NZ)
        py = lax.rem(y + lax.rem(k // NZ, NY), NY)
        d = at(px, pz, py)
        pltpu.make_async_remote_copy(
            src_ref=tags.at[d], dst_ref=got_tags.at[me], send_sem=t_send, recv_sem=t_recv,
            device_id=(other, d), device_id_type=MESH,
        ).start()
        pltpu.make_async_remote_copy(
            src_ref=packed.at[d], dst_ref=got.at[me], send_sem=s_send, recv_sem=s_recv,
            device_id=(other, d), device_id_type=MESH,
        ).start()

    def send_tiles(first, count):
        def one(k, carry):
            send_one(k)
            return carry

        lax.fori_loop(first, first + count, one, 0)

    send_tiles(0, 24)

    pre_row = pre_ref[...].astype(F32)
    eval_row = eval_ref[...].astype(F32)
    dof_row = dof_ref[...].astype(F32)
    dof_col = jnp.transpose(jnp.broadcast_to(dof_row, (ROWS, ROWS)))
    lane512 = lax.broadcasted_iota(jnp.int32, (ROWS, ND), 1).astype(F32)
    sub512 = lax.broadcasted_iota(jnp.int32, (ND, ROWS), 0).astype(F32)
    picks = []
    for g in range(2):
        halves = []
        for a in range(2):
            here = dof_col[:, 0:1] * 2.0 + (a - g * ND)
            halves.append(jnp.where(lane512 == here, 1.0, 0.0).astype(BF))
            there = dof_row * 2.0 + (a - g * ND)
            scat[g, :, a * ROWS:(a + 1) * ROWS] = jnp.where(sub512 == there, 1.0, 0.0).astype(BF)
        picks.append(jnp.concatenate(halves, axis=0))
    sub128 = lax.broadcasted_iota(jnp.int32, (ROWS, ROWS), 0).astype(F32)
    weights32 = jnp.where(sub128 == eval_row, pre_row, 0.0)
    weights = weights32.astype(BF)
    load = jnp.broadcast_to(jnp.sum(weights32, axis=1, keepdims=True), (NDEV, PTS))
    load_hi = load.astype(BF)
    psend[1, :, :, 18] = load_hi.reshape(4, 2, 16, PTS)
    psend[1, :, :, 19] = (load - load_hi.astype(F32)).astype(BF).reshape(4, 2, 16, PTS)
    loads[1].wait()

    def comps(g, c, n):
        tiles = []
        for i in range(n):
            item = g * NC + c + i
            parts = [edge[item].reshape(NIF, PTS), inner[item].reshape(ND - NIF, PTS)]
            tiles.append(jnp.concatenate(parts, axis=0))
        return tiles[0] if n == 1 else jnp.concatenate(tiles, axis=1)

    def gather(c, n, half):
        got_rows = dot(picks[0], comps(0, c, n)) + dot(picks[1], comps(1, c, n))
        narrow = got_rows.astype(BF)
        for i in range(n):
            pay[c + i] = got_rows[:, i * PTS:(i + 1) * PTS]
        for a in range(2):
            summed = dot(weights, narrow[a * ROWS:(a + 1) * ROWS]).astype(BF)
            for i in range(n):
                part = summed[:, i * PTS:(i + 1) * PTS].reshape(4, 2, 16, PTS)
                psend[half, :, :, (c + i) * 2 + a - 20 * half] = part

    def gather_pair(half, i, carry):
        send_one(24 + 2 * i)
        gather(2 * i, 2, half)
        send_one(25 + 2 * i)
        return carry

    lax.fori_loop(0, 5, functools.partial(gather_pair, 0), 0)
    lax.fori_loop(5, 9, functools.partial(gather_pair, 1), 0)
    gather(18, 1, 1)

    def push(src, dst, step, device):
        pltpu.make_async_remote_copy(
            src_ref=src, dst_ref=dst, send_sem=r_send.at[step], recv_sem=r_recv.at[step],
            device_id=device, device_id_type=MESH,
        ).start()

    def arrived(ref, step):
        pltpu.make_async_copy(ref, ref, r_recv.at[step]).wait()

    def left(ref, step):
        pltpu.make_async_copy(ref, ref, r_send.at[step]).wait()

    mine = ((x, y), (y, x))
    peers = ((x_peer, y_peer), (y_peer, x_peer))

    def device(half, turn, k):
        if half == turn:
            return sec, at(x_peer(k), z, y)
        return sec, at(x, z, y_peer(k))

    for k in range(1, 4):
        for half in range(2):
            push(psend.at[half, peers[half][0](k)], rx.at[half, mine[half][0]], 0, device(half, 0, k))
    loads[2].wait()
    loads[3].wait()
    for g in range(2):
        stm[g, 0:ND] = jnp.transpose(stiff[g])
        stm[g, ND:2 * ND] = jnp.transpose(mass[g])

    soft = 0.01 / (freq[...] * freq[...])

    def contact(b, carry):
        for i in range(3):
            send_one(42 + 3 * b + i)
        low = pl.multiple_of(b * 8, 8)
        sides = []
        for a in range(2):
            lines = [pay[c, pl.ds(a * ROWS + low, 8), :] for c in range(1, NC)]
            sides.append(jnp.concatenate(lines, axis=0))
        values = jnp.concatenate(sides, axis=1).astype(BF)
        speed = dot(slope_t[...], jnp.concatenate([values, values], axis=0))
        one, two = speed[:, 0:PTS], speed[:, PTS:2 * PTS]
        inverse = lax.rsqrt(one * one + two * two + soft)
        slide = jnp.concatenate([(one * inverse).astype(BF), (two * inverse).astype(BF)], axis=1)
        both = dot(proj_t[...], slide)
        total = both[0:8 * NC] + both[8 * NC:16 * NC]
        for c in range(NC):
            for a in range(2):
                harm[c, pl.ds(a * ROWS + low, 8), :] = total[8 * c:8 * c + 8, a * PTS:(a + 1) * PTS]
        return carry

    lax.fori_loop(0, 9, contact, 0)

    def split(total):
        high = total.astype(BF)
        return high, (total - high.astype(F32)).astype(BF)

    arrived(rx.at[:, 0:3], 0)
    for half in range(2):
        whole = psend[half, mine[half][0]].astype(F32)
        for k in range(1, 4):
            whole = whole + rx[half, peers[half][0](k)].astype(F32)
        for g in range(2):
            for part in range(2):
                ysend[half, 2 * g + part] = whole[g, 10 * part:10 * part + 10].astype(BF)
        if half == 1:
            high, low = split(whole[:, 18] + whole[:, 19])
            for g in range(2):
                ysend[1, 2 * g + 1, 8] = high[g]
                ysend[1, 2 * g + 1, 9] = low[g]
    for k in range(1, 4):
        for half in range(2):
            push(ysend.at[half, peers[half][1](k)], ry.at[half, mine[half][1]], 1, device(half, 1, k))
    lax.fori_loop(9, 13, contact, 0)

    odd = lax.rem(x, 2) == 1
    arrived(ry.at[:, 0:3], 1)
    zsend[5:8] = jnp.zeros((3, 4, 16, PTS), BF)
    for half in range(2):
        whole = ysend[half, mine[half][1]].astype(F32)
        for k in range(1, 4):
            whole = whole + ry[half, peers[half][1](k)].astype(F32)
        for part in range(5):
            zsend[part, 2 * half:2 * half + 2] = whole[2 * part:2 * part + 2].astype(BF)
        if half == 1:
            high, low = split(whole[8] + whole[9])
            zsend[4, 2] = jnp.where(odd, high.astype(F32), whole[8]).astype(BF)
            zsend[4, 3] = jnp.where(odd, low.astype(F32), whole[9]).astype(BF)
    for k in range(1, NZ):
        push(zsend.at[z_peer(k)], rz.at[z], 2, (sec, at(x, z_peer(k), y)))
    lax.fori_loop(13, 16, contact, 0)

    def balance(g, c, n):
        both = dot(stm[g], comps(g, c, n))
        for i in range(n):
            h = jnp.where(c + i <= HARM, c + i, c + i - HARM)
            scaled = jnp.asarray(h, jnp.int32).astype(F32) * freq[...]
            lanes = slice(i * PTS, (i + 1) * PTS)
            resid[g * NC + c + i] = both[0:ND, lanes] - (scaled * scaled) * both[ND:2 * ND, lanes]

    def balance_pair(g, i, carry):
        send_one(90 + 18 * g + 2 * i)
        balance(g, 2 * i, 2)
        send_one(91 + 18 * g + 2 * i)
        return carry

    arrived(rz.at[0:7], 2)
    whole = zsend[z].astype(F32)
    for k in range(1, NZ):
        whole = whole + rz[z_peer(k)].astype(F32)
    high, low = split(whole[2] + whole[3])
    here = jnp.logical_and(odd, z == 4)
    agz[z, 0:2] = whole[0:2].astype(BF)
    agz[z, 2] = jnp.where(here, high.astype(F32), whole[2]).astype(BF)
    agz[z, 3] = jnp.where(here, low.astype(F32), whole[3]).astype(BF)
    for k in range(1, NZ):
        push(agz.at[z], agz.at[z], 3, (sec, at(x, z_peer(k), y)))
    lax.fori_loop(0, 5, functools.partial(balance_pair, 0), 0)

    arrived(agz.at[0:7], 3)
    for half in range(2):
        agy[half, mine[half][1]] = agz[0:5, 2 * half:2 * half + 2].reshape(10, 16, PTS)
        for k in range(1, 4):
            slot = agy.at[half, mine[half][1]]
            push(slot, slot, 4, device(half, 1, k))
    lax.fori_loop(5, 9, functools.partial(balance_pair, 0), 0)
    balance(0, 18, 1)

    arrived(agy.at[:, 0:3], 4)
    for half in range(2):
        agx[half, mine[half][0]] = agy[half].reshape(2, 20, 16, PTS)
        for k in range(1, 4):
            slot = agx.at[half, mine[half][0]]
            push(slot, slot, 5, device(half, 0, k))
    lax.fori_loop(0, 9, functools.partial(balance_pair, 1), 0)
    balance(1, 18, 1)
    send_tiles(126, 2)
    arrived(agx.at[:, 0:3], 5)

    lane128 = lax.broadcasted_iota(jnp.int32, (ROWS, ROWS), 1).astype(F32)
    eval_col = jnp.transpose(jnp.broadcast_to(eval_row, (ROWS, ROWS)))
    pre_col = jnp.transpose(jnp.broadcast_to(pre_row, (ROWS, ROWS)))
    choose = jnp.where(lane128 == eval_col, 1.0, 0.0).astype(BF)

    def joints(half, k):
        return agx[half, :, :, k].reshape(NDEV, PTS)

    loaded = dot(choose, jnp.concatenate([joints(1, 18), joints(1, 19)], axis=1))
    per_load = 1.0 / (loaded[:, 0:PTS] + loaded[:, PTS:2 * PTS])
    pressed = pre_col * (FRICTION * ROWS) * per_load

    def forces(half, c, carry):
        k = 2 * c - 20 * half
        mean = dot(choose, jnp.concatenate([joints(half, k), joints(half, k + 1)], axis=1))
        for a in range(2):
            rows = slice(a * ROWS, (a + 1) * ROWS)
            away = pay[c, rows, :] - mean[:, a * PTS:(a + 1) * PTS] * per_load
            force[c, rows, :] = (STIFF * away + pressed * harm[c, rows, :]).astype(BF)
        return carry

    lax.fori_loop(0, 10, functools.partial(forces, 0), 0)
    lax.fori_loop(10, NC, functools.partial(forces, 1), 0)

    def finish(g, c, n):
        lines = [force[c + i] for i in range(n)]
        added = dot(scat[g], lines[0] if n == 1 else jnp.concatenate(lines, axis=1))
        for i in range(n):
            item = g * NC + c + i
            value = resid[item] + added[:, i * PTS:(i + 1) * PTS]
            near[item] = value[0:NIF]
            far[item] = value[NIF:ND].astype(BF)

    def finish_pair(g, i, carry):
        finish(g, 2 * i, 2)
        return carry

    stores = []
    for g in range(2):
        lax.fori_loop(0, 9, functools.partial(finish_pair, g), 0)
        finish(g, 18, 1)
        block = pl.ds(g * NC, NC)
        stores.append(pltpu.make_async_copy(far.at[block], part_b.at[block], l_sem.at[5 + g]))
        stores.append(pltpu.make_async_copy(near.at[block], part_f.at[block], l_sem.at[7 + g]))
        stores[-2].start()
        stores[-1].start()

    left(rx.at[:, 0:3], 0)
    left(ry.at[:, 0:3], 1)
    left(rz.at[0:7], 2)
    left(agz.at[0:7], 3)
    left(agy.at[:, 0:3], 4)
    left(agx.at[:, 0:3], 5)
    for store in stores:
        store.wait()
    pltpu.make_async_copy(packed, packed, s_send).wait()
    pltpu.make_async_copy(tags, tags, t_send).wait()
    pltpu.make_async_copy(got_tags, got_tags, t_recv).wait()
    pltpu.make_async_copy(got, got, s_recv).wait()


def last_kernel(
    got_h, tags_h, part_f, part_b, coupling, out_h,
    got, tags, near, out, glued, link, sems,
):
    tag_copy = pltpu.make_async_copy(tags_h, tags, sems.at[0])
    got_copy = pltpu.make_async_copy(got_h, got, sems.at[1])
    near_copy = pltpu.make_async_copy(part_f, near, sems.at[2])
    tag_copy.start()
    got_copy.start()
    near_copy.start()
    fars = []
    for g in range(2):
        block = pl.ds(g * NC, NC)
        fars.append(pltpu.make_async_copy(part_b.at[block], out.at[block, NIF:ND], sems.at[3 + g]))
        fars[g].start()
    glued[...] = jnp.zeros_like(glued)
    link[...] = jnp.zeros_like(link)
    for g in range(2):
        for q in range(4):
            span = slice(32 * q, 32 * q + 32)
            link[g, span, span] = jnp.transpose(coupling[g, q].astype(F32)).astype(BF)
    tag_copy.wait()
    got_copy.wait()

    def add(d, carry):
        for s in range(2):
            slot = tags[d, 0, 64 * s]
            glued[s, slot] = glued[s, slot] + got[d, 32 * s:32 * s + 32, :].astype(F32)
        return carry

    lax.fori_loop(0, NDEV, add, 0, unroll=4)
    near_copy.wait()

    def item(g, c):
        span = pl.ds((g * NC + c) * 4, 4)
        return (glued[0, span] + glued[1, span]).reshape(NIF, PTS).astype(BF)

    def finish(g, c, n):
        tiles = [item(g, c + i) for i in range(n)]
        added = dot(link[g], tiles[0] if n == 1 else jnp.concatenate(tiles, axis=1))
        for i in range(n):
            at = g * NC + c + i
            out[at, 0:NIF] = (near[at] + added[:, i * PTS:(i + 1) * PTS]).astype(BF)

    def finish_pair(g, i, carry):
        finish(g, 2 * i, 2)
        return carry

    stores = []
    for g in range(2):
        lax.fori_loop(0, 9, functools.partial(finish_pair, g), 0)
        finish(g, 18, 1)
        block = pl.ds(g * NC, NC)
        fars[g].wait()
        stores.append(pltpu.make_async_copy(out.at[block], out_h.at[block], sems.at[5 + g]))
        stores[g].start()
    for store in stores:
        store.wait()


def body(modal, stiffness, mass, freq, coupling, route, target, contact_dof, evaluator, preload):
    slope_table, proj_table = fourier_tables()
    vmem = pl.BlockSpec(memory_space=pltpu.VMEM)
    anywhere = pl.BlockSpec(memory_space=pl.ANY)
    dma = pltpu.SemaphoreType.DMA
    part_f, part_b, got, got_tags = pl.pallas_call(
        main_kernel,
        out_shape=(
            jax.ShapeDtypeStruct((2 * NC, NIF, PTS), F32),
            jax.ShapeDtypeStruct((2 * NC, ND - NIF, PTS), BF),
            jax.ShapeDtypeStruct((NDEV, 64, PTS), BF),
            jax.ShapeDtypeStruct((NDEV, 1, 128), jnp.int32),
        ),
        in_specs=[anywhere] * 3 + [vmem] * 8,
        out_specs=(anywhere,) * 4,
        scratch_shapes=[
            pltpu.VMEM((2 * NC, 4, 32, PTS), BF),
            pltpu.VMEM((2 * NC, 12, 32, PTS), BF),
            pltpu.VMEM((2, ND, ND), BF),
            pltpu.VMEM((2, ND, ND), BF),
            pltpu.VMEM((NDEV, 128), jnp.int32),
            pltpu.SMEM((NDEV, 128), jnp.int32),
            pltpu.VMEM((NDEV, 1, 128), jnp.int32),
            pltpu.VMEM((NDEV, 64, PTS), BF),
            pltpu.VMEM((2, 4, 2, 20, 16, PTS), BF),
            pltpu.VMEM((2, 4, 2, 20, 16, PTS), BF),
            pltpu.VMEM((2, 4, 10, 16, PTS), BF),
            pltpu.VMEM((2, 4, 10, 16, PTS), BF),
            pltpu.VMEM((NZ, 4, 16, PTS), BF),
            pltpu.VMEM((NZ, 4, 16, PTS), BF),
            pltpu.VMEM((NZ, 4, 16, PTS), BF),
            pltpu.VMEM((2, 4, 10, 16, PTS), BF),
            pltpu.VMEM((2, 4, 2, 20, 16, PTS), BF),
            pltpu.VMEM((NC, 2 * ROWS, PTS), F32),
            pltpu.VMEM((NC, 2 * ROWS, PTS), F32),
            pltpu.VMEM((NC, 2 * ROWS, PTS), BF),
            pltpu.VMEM((2 * NC, ND, PTS), F32),
            pltpu.VMEM((2, 2 * ND, ND), BF),
            pltpu.VMEM((2, ND, 2 * ROWS), BF),
            pltpu.VMEM((2 * NC, NIF, PTS), F32),
            pltpu.VMEM((2 * NC, ND - NIF, PTS), BF),
            dma((9,)), dma, dma, dma, dma, dma((6,)), dma((6,)),
        ],
        compiler_params=pltpu.CompilerParams(
            collective_id=1, has_side_effects=True, vmem_limit_bytes=58 << 20
        ),
    )(modal.reshape(2 * NC, 16, 32, PTS), stiffness[0], mass[0], freq.reshape(1, PTS),
      preload, evaluator.reshape(1, ROWS), contact_dof, route.reshape(1, TILES), target,
      jnp.asarray(slope_table), jnp.asarray(proj_table))

    out = pl.pallas_call(
        last_kernel,
        out_shape=jax.ShapeDtypeStruct((2 * NC, ND, PTS), BF),
        in_specs=[anywhere] * 4 + [vmem],
        out_specs=anywhere,
        scratch_shapes=[
            pltpu.VMEM((NDEV, 64, PTS), BF),
            pltpu.SMEM((NDEV, 1, 128), jnp.int32),
            pltpu.VMEM((2 * NC, NIF, PTS), F32),
            pltpu.VMEM((2 * NC, ND, PTS), BF),
            pltpu.VMEM((2, TILES + 1, 32, PTS), F32),
            pltpu.VMEM((2, NIF, NIF), BF),
            dma((7,)),
        ],
        compiler_params=pltpu.CompilerParams(vmem_limit_bytes=58 << 20),
    )(got, got_tags, part_f, part_b, coupling[0])
    return out.reshape(1, 2, NC, ND, PTS)


def solution(mesh):
    placed = (
        P("section", "diam", None, None, None),
        P("section", "diam", None, None),
        P("section", "diam", None, None),
        P(),
        P("section", "diam", None, None, None),
        P("section", "diam", None),
        P("section", "diam"),
        P("section", "diam"),
        P("section", "diam", None),
        P("section", "diam"),
    )
    return jax.shard_map(
        body,
        mesh=mesh,
        in_specs=placed,
        out_specs=P("section", "diam", None, None, None),
        check_vma=False,
    )
```

```python
import functools
import math

import jax
import jax.numpy as jnp
import ml_dtypes
import numpy as np
from jax import lax
from jax.experimental import pallas as pl
from jax.experimental.pallas import tpu as pltpu
from jax.sharding import PartitionSpec as P

HARM = 9
NC = 19
ND = 512
NIF = 128
NT = 128
PTS = 128
NX, NZ, NY = 4, 8, 4
NDEV = 128
TILES = 152
ROWS = 128
STIFF = 0.3
FRICTION = 0.6
MESH = pl.DeviceIdType.MESH
BF = jnp.bfloat16
F32 = jnp.float32


def high_low(table):
    high = table.astype(ml_dtypes.bfloat16)
    low = (table - high.astype(np.float64)).astype(ml_dtypes.bfloat16)
    return high, low


def fourier_tables():
    comp = np.arange(NC)
    order = np.where(comp <= HARM, comp, comp - HARM).astype(np.float64)
    phase = order[:, None] * (np.arange(NT) * (2.0 * math.pi / NT))[None, :]
    sine = (comp > HARM)[:, None]
    slope = np.where(sine, order[:, None] * np.cos(phase), -order[:, None] * np.sin(phase))
    shape = np.where(sine, np.sin(phase), np.cos(phase))
    weight = np.where(comp == 0, 1.0 / NT, 2.0 / NT)
    eye = np.eye(8)
    s_hi, s_lo = high_low(slope[1:].T)
    p_hi, p_lo = high_low(shape * weight[:, None])
    spread = lambda t: np.kron(t.astype(np.float64), eye).astype(ml_dtypes.bfloat16)
    slope_table = np.concatenate([spread(s_hi), spread(s_lo)], axis=1)
    proj_table = np.concatenate([spread(p_hi), spread(p_lo)], axis=0)
    return slope_table, proj_table


def dot(a, b):
    return jnp.dot(a, b, preferred_element_type=F32)


def main_kernel(
    modal_h, stiff_h, mass_h, freq, pre_ref, eval_ref, dof_ref, route_ref, target_ref,
    slope_t, proj_t,
    part_f, part_b, got, got_tags,
    edge, inner, stiff, mass, source, source_s, tags, packed,
    psend, rx, ysend, ry, zsend, rz, agz, agy, agx,
    pay, harm, force, resid, stm, scat, near, far,
    l_sem, s_send, s_recv, t_send, t_recv, r_send, r_recv,
):
    sec = lax.axis_index("section")
    me = lax.axis_index("diam")
    other = 1 - sec
    x = me // (NZ * NY)
    z = lax.rem(me // NY, NZ)
    y = lax.rem(me, NY)

    def at(px, pz, py):
        return (px * NZ + pz) * NY + py

    def x_peer(k):
        return lax.rem(x + k, NX)

    def y_peer(k):
        return lax.rem(y + k, NY)

    def z_peer(k):
        return lax.rem(z + k, NZ)

    loads = [
        pltpu.make_async_copy(modal_h.at[:, 0:4], edge, l_sem.at[0]),
        pltpu.make_async_copy(modal_h.at[:, 4:16], inner, l_sem.at[1]),
        pltpu.make_async_copy(stiff_h, stiff, l_sem.at[2]),
        pltpu.make_async_copy(mass_h, mass, l_sem.at[3]),
    ]
    for load in loads:
        load.start()

    barrier = pltpu.get_barrier_semaphore()

    def hail(k, carry):
        pl.semaphore_signal(barrier, inc=1, device_id=(other, k), device_id_type=MESH)
        return carry

    lax.fori_loop(0, NDEV, hail, 0)
    for k in range(1, NX):
        pl.semaphore_signal(barrier, inc=1, device_id=(sec, at(x_peer(k), z, y)), device_id_type=MESH)
    for k in range(1, NY):
        pl.semaphore_signal(barrier, inc=1, device_id=(sec, at(x, z, y_peer(k))), device_id_type=MESH)
    for k in range(1, NZ):
        pl.semaphore_signal(barrier, inc=1, device_id=(sec, at(x, z_peer(k), y)), device_id_type=MESH)

    spot = lax.broadcasted_iota(jnp.int32, (NDEV, TILES), 1)
    named = route_ref[...] == lax.broadcasted_iota(jnp.int32, (NDEV, TILES), 0)
    key = (spot * 256 + target_ref[...])
    first = jnp.min(jnp.where(named, key, 1 << 20), axis=1, keepdims=True)
    final = jnp.max(jnp.where(named, key, -1), axis=1, keepdims=True)
    none = jnp.full_like(first, TILES)
    one_key = jnp.where(first < (1 << 20), first, none)
    two_key = jnp.where((final >= 0) & (final != first), final, none)
    lane = lax.broadcasted_iota(jnp.int32, (NDEV, 128), 1)
    keys = jnp.where(lane < 64, one_key, two_key)
    source[...] = jnp.right_shift(keys, 8)
    tags[...] = jnp.bitwise_and(keys, 255).reshape(NDEV, 1, 128)
    listing = pltpu.make_async_copy(source, source_s, l_sem.at[4])
    listing.start()

    pre_row = pre_ref[...].astype(F32)
    eval_row = eval_ref[...].astype(F32)
    dof_row = dof_ref[...].astype(F32)
    dof_col = jnp.transpose(jnp.broadcast_to(dof_row, (ROWS, ROWS)))
    lane512 = lax.broadcasted_iota(jnp.int32, (ROWS, ND), 1).astype(F32)
    sub512 = lax.broadcasted_iota(jnp.int32, (ND, ROWS), 0).astype(F32)
    picks = []
    for g in range(2):
        halves = []
        for a in range(2):
            here = dof_col[:, 0:1] * 2.0 + (a - g * ND)
            halves.append(jnp.where(lane512 == here, 1.0, 0.0).astype(BF))
            there = dof_row * 2.0 + (a - g * ND)
            scat[g, :, a * ROWS:(a + 1) * ROWS] = jnp.where(sub512 == there, 1.0, 0.0).astype(BF)
        picks.append(jnp.concatenate(halves, axis=0))
    sub128 = lax.broadcasted_iota(jnp.int32, (ROWS, ROWS), 0).astype(F32)
    weights32 = jnp.where(sub128 == eval_row, pre_row, 0.0)
    weights = weights32.astype(BF)
    load = jnp.broadcast_to(jnp.sum(weights32, axis=1, keepdims=True), (NDEV, PTS))
    load_hi = load.astype(BF)
    psend[1, :, :, 18] = load_hi.reshape(4, 2, 16, PTS)
    psend[1, :, :, 19] = (load - load_hi.astype(F32)).astype(BF).reshape(4, 2, 16, PTS)
    loads[0].wait()
    loads[1].wait()

    def comps(g, c, n):
        tiles = []
        for i in range(n):
            item = g * NC + c + i
            parts = [edge[item].reshape(NIF, PTS), inner[item].reshape(ND - NIF, PTS)]
            tiles.append(jnp.concatenate(parts, axis=0))
        return tiles[0] if n == 1 else jnp.concatenate(tiles, axis=1)

    def gather(c, n, half):
        got_rows = dot(picks[0], comps(0, c, n)) + dot(picks[1], comps(1, c, n))
        narrow = got_rows.astype(BF)
        for i in range(n):
            pay[c + i] = got_rows[:, i * PTS:(i + 1) * PTS]
        for a in range(2):
            summed = dot(weights, narrow[a * ROWS:(a + 1) * ROWS]).astype(BF)
            for i in range(n):
                part = summed[:, i * PTS:(i + 1) * PTS].reshape(4, 2, 16, PTS)
                psend[half, :, :, (c + i) * 2 + a - 20 * half] = part

    def gather_pair(half, i, carry):
        gather(2 * i, 2, half)
        return carry

    lax.fori_loop(0, 5, functools.partial(gather_pair, 0), 0)
    lax.fori_loop(5, 9, functools.partial(gather_pair, 1), 0)
    gather(18, 1, 1)

    pl.semaphore_wait(barrier, NDEV + NX + NY + NZ - 3)

    def push(src, dst, step, device):
        pltpu.make_async_remote_copy(
            src_ref=src, dst_ref=dst, send_sem=r_send.at[step], recv_sem=r_recv.at[step],
            device_id=device, device_id_type=MESH,
        ).start()

    def arrived(ref, step):
        pltpu.make_async_copy(ref, ref, r_recv.at[step]).wait()

    def left(ref, step):
        pltpu.make_async_copy(ref, ref, r_send.at[step]).wait()

    mine = ((x, y), (y, x))
    peers = ((x_peer, y_peer), (y_peer, x_peer))

    def device(half, turn, k):
        if half == turn:
            return sec, at(x_peer(k), z, y)
        return sec, at(x, z, y_peer(k))

    for k in range(1, 4):
        for half in range(2):
            push(psend.at[half, peers[half][0](k)], rx.at[half, mine[half][0]], 0, device(half, 0, k))

    listing.wait()

    def tile(t):
        return edge[jnp.right_shift(t, 2), jnp.bitwise_and(t, 3)]

    def pack(d, carry):
        packed[d, 0:32, :] = tile(source_s[d, 0])
        packed[d, 32:64, :] = tile(source_s[d, 64])
        return carry

    lax.fori_loop(0, NDEV, pack, 0)
    def send_one(k):
        px = lax.rem(x + k // (NZ * NY), NX)
        pz = lax.rem(z + lax.rem(k, NZ), NZ)
        py = lax.rem(y + lax.rem(k // NZ, NY), NY)
        d = at(px, pz, py)
        pltpu.make_async_remote_copy(
            src_ref=tags.at[d], dst_ref=got_tags.at[me], send_sem=t_send, recv_sem=t_recv,
            device_id=(other, d), device_id_type=MESH,
        ).start()
        pltpu.make_async_remote_copy(
            src_ref=packed.at[d], dst_ref=got.at[me], send_sem=s_send, recv_sem=s_recv,
            device_id=(other, d), device_id_type=MESH,
        ).start()

    def send_tiles(first, count):
        def one(k, carry):
            send_one(k)
            return carry

        lax.fori_loop(first, first + count, one, 0)

    send_tiles(0, 10)
    loads[2].wait()
    loads[3].wait()
    for g in range(2):
        stm[g, 0:ND] = jnp.transpose(stiff[g])
        stm[g, ND:2 * ND] = jnp.transpose(mass[g])

    soft = 0.01 / (freq[...] * freq[...])

    def contact(b, carry):
        for i in range(2):
            send_one(10 + 2 * b + i)
        low = pl.multiple_of(b * 8, 8)
        sides = []
        for a in range(2):
            lines = [pay[c, pl.ds(a * ROWS + low, 8), :] for c in range(1, NC)]
            sides.append(jnp.concatenate(lines, axis=0))
        values = jnp.concatenate(sides, axis=1).astype(BF)
        speed = dot(slope_t[...], jnp.concatenate([values, values], axis=0))
        one, two = speed[:, 0:PTS], speed[:, PTS:2 * PTS]
        inverse = lax.rsqrt(one * one + two * two + soft)
        slide = jnp.concatenate([(one * inverse).astype(BF), (two * inverse).astype(BF)], axis=1)
        both = dot(proj_t[...], slide)
        total = both[0:8 * NC] + both[8 * NC:16 * NC]
        for c in range(NC):
            for a in range(2):
                harm[c, pl.ds(a * ROWS + low, 8), :] = total[8 * c:8 * c + 8, a * PTS:(a + 1) * PTS]
        return carry

    lax.fori_loop(0, 8, contact, 0, unroll=2)

    def split(total):
        high = total.astype(BF)
        return high, (total - high.astype(F32)).astype(BF)

    send_tiles(42, 4)
    arrived(rx.at[:, 0:3], 0)
    for half in range(2):
        whole = psend[half, mine[half][0]].astype(F32)
        for k in range(1, 4):
            whole = whole + rx[half, peers[half][0](k)].astype(F32)
        for g in range(2):
            for part in range(2):
                ysend[half, 2 * g + part] = whole[g, 10 * part:10 * part + 10].astype(BF)
        if half == 1:
            high, low = split(whole[:, 18] + whole[:, 19])
            for g in range(2):
                ysend[1, 2 * g + 1, 8] = high[g]
                ysend[1, 2 * g + 1, 9] = low[g]
    for k in range(1, 4):
        for half in range(2):
            push(ysend.at[half, peers[half][1](k)], ry.at[half, mine[half][1]], 1, device(half, 1, k))
    lax.fori_loop(8, 12, contact, 0, unroll=2)

    odd = lax.rem(x, 2) == 1
    send_tiles(46, 4)
    arrived(ry.at[:, 0:3], 1)
    zsend[5:8] = jnp.zeros((3, 4, 16, PTS), BF)
    for half in range(2):
        whole = ysend[half, mine[half][1]].astype(F32)
        for k in range(1, 4):
            whole = whole + ry[half, peers[half][1](k)].astype(F32)
        for part in range(5):
            zsend[part, 2 * half:2 * half + 2] = whole[2 * part:2 * part + 2].astype(BF)
        if half == 1:
            high, low = split(whole[8] + whole[9])
            zsend[4, 2] = jnp.where(odd, high.astype(F32), whole[8]).astype(BF)
            zsend[4, 3] = jnp.where(odd, low.astype(F32), whole[9]).astype(BF)
    for k in range(1, NZ):
        push(zsend.at[z_peer(k)], rz.at[z], 2, (sec, at(x, z_peer(k), y)))
    lax.fori_loop(12, 16, contact, 0, unroll=2)

    def balance(g, c, n):
        both = dot(stm[g], comps(g, c, n))
        for i in range(n):
            h = jnp.where(c + i <= HARM, c + i, c + i - HARM)
            scaled = jnp.asarray(h, jnp.int32).astype(F32) * freq[...]
            lanes = slice(i * PTS, (i + 1) * PTS)
            resid[g * NC + c + i] = both[0:ND, lanes] - (scaled * scaled) * both[ND:2 * ND, lanes]

    def balance_pair(g, i, carry):
        if g == 0:
            send_one(62 + 2 * i)
            send_one(63 + 2 * i)
        balance(g, 2 * i, 2)
        return carry

    send_tiles(50, 4)
    arrived(rz.at[0:7], 2)
    whole = zsend[z].astype(F32)
    for k in range(1, NZ):
        whole = whole + rz[z_peer(k)].astype(F32)
    high, low = split(whole[2] + whole[3])
    here = jnp.logical_and(odd, z == 4)
    agz[z, 0:2] = whole[0:2].astype(BF)
    agz[z, 2] = jnp.where(here, high.astype(F32), whole[2]).astype(BF)
    agz[z, 3] = jnp.where(here, low.astype(F32), whole[3]).astype(BF)
    for k in range(1, NZ):
        push(agz.at[z], agz.at[z], 3, (sec, at(x, z_peer(k), y)))
    lax.fori_loop(0, 5, functools.partial(balance_pair, 0), 0)

    send_tiles(54, 4)
    arrived(agz.at[0:7], 3)
    for half in range(2):
        agy[half, mine[half][1]] = agz[0:5, 2 * half:2 * half + 2].reshape(10, 16, PTS)
        for k in range(1, 4):
            slot = agy.at[half, mine[half][1]]
            push(slot, slot, 4, device(half, 1, k))
    lax.fori_loop(5, 9, functools.partial(balance_pair, 0), 0)
    balance(0, 18, 1)

    send_tiles(58, 4)
    arrived(agy.at[:, 0:3], 4)
    for half in range(2):
        agx[half, mine[half][0]] = agy[half].reshape(2, 20, 16, PTS)
        for k in range(1, 4):
            slot = agx.at[half, mine[half][0]]
            push(slot, slot, 5, device(half, 0, k))
    send_tiles(80, 48)
    lax.fori_loop(0, 9, functools.partial(balance_pair, 1), 0, unroll=3)
    balance(1, 18, 1)
    arrived(agx.at[:, 0:3], 5)

    lane128 = lax.broadcasted_iota(jnp.int32, (ROWS, ROWS), 1).astype(F32)
    eval_col = jnp.transpose(jnp.broadcast_to(eval_row, (ROWS, ROWS)))
    pre_col = jnp.transpose(jnp.broadcast_to(pre_row, (ROWS, ROWS)))
    choose = jnp.where(lane128 == eval_col, 1.0, 0.0).astype(BF)

    def joints(half, k):
        return agx[half, :, :, k].reshape(NDEV, PTS)

    loaded = dot(choose, jnp.concatenate([joints(1, 18), joints(1, 19)], axis=1))
    per_load = 1.0 / (loaded[:, 0:PTS] + loaded[:, PTS:2 * PTS])
    pressed = pre_col * (FRICTION * ROWS) * per_load

    def forces(half, c, carry):
        k = 2 * c - 20 * half
        mean = dot(choose, jnp.concatenate([joints(half, k), joints(half, k + 1)], axis=1))
        for a in range(2):
            rows = slice(a * ROWS, (a + 1) * ROWS)
            away = pay[c, rows, :] - mean[:, a * PTS:(a + 1) * PTS] * per_load
            force[c, rows, :] = (STIFF * away + pressed * harm[c, rows, :]).astype(BF)
        return carry

    lax.fori_loop(0, 10, functools.partial(forces, 0), 0, unroll=2)
    lax.fori_loop(10, NC, functools.partial(forces, 1), 0, unroll=3)

    def finish(g, c, n):
        lines = [force[c + i] for i in range(n)]
        added = dot(scat[g], lines[0] if n == 1 else jnp.concatenate(lines, axis=1))
        for i in range(n):
            item = g * NC + c + i
            value = resid[item] + added[:, i * PTS:(i + 1) * PTS]
            near[item] = value[0:NIF]
            far[item] = value[NIF:ND].astype(BF)

    def finish_pair(g, i, carry):
        finish(g, 2 * i, 2)
        return carry

    stores = []
    for g in range(2):
        lax.fori_loop(0, 9, functools.partial(finish_pair, g), 0, unroll=3)
        finish(g, 18, 1)
        block = pl.ds(g * NC, NC)
        stores.append(pltpu.make_async_copy(far.at[block], part_b.at[block], l_sem.at[5 + g]))
        stores.append(pltpu.make_async_copy(near.at[block], part_f.at[block], l_sem.at[7 + g]))
        stores[-2].start()
        stores[-1].start()

    left(rx.at[:, 0:3], 0)
    left(ry.at[:, 0:3], 1)
    left(rz.at[0:7], 2)
    left(agz.at[0:7], 3)
    left(agy.at[:, 0:3], 4)
    left(agx.at[:, 0:3], 5)
    for store in stores:
        store.wait()
    pltpu.make_async_copy(packed, packed, s_send).wait()
    pltpu.make_async_copy(tags, tags, t_send).wait()
    pltpu.make_async_copy(got_tags, got_tags, t_recv).wait()
    pltpu.make_async_copy(got, got, s_recv).wait()


def last_kernel(
    got_h, tags_h, part_f, part_b, coupling, out_h,
    got, tags, near, out, glued, link, sems,
):
    tag_copy = pltpu.make_async_copy(tags_h, tags, sems.at[0])
    got_copy = pltpu.make_async_copy(got_h, got, sems.at[1])
    near_copy = pltpu.make_async_copy(part_f, near, sems.at[2])
    tag_copy.start()
    got_copy.start()
    near_copy.start()
    fars = []
    for g in range(2):
        block = pl.ds(g * NC, NC)
        fars.append(pltpu.make_async_copy(part_b.at[block], out.at[block, NIF:ND], sems.at[3 + g]))
        fars[g].start()
    glued[...] = jnp.zeros_like(glued)
    link[...] = jnp.zeros_like(link)
    for g in range(2):
        for q in range(4):
            span = slice(32 * q, 32 * q + 32)
            link[g, span, span] = jnp.transpose(coupling[g, q].astype(F32)).astype(BF)
    tag_copy.wait()
    got_copy.wait()

    def add(d, carry):
        for s in range(2):
            slot = tags[d, 0, 64 * s]
            glued[s, slot] = glued[s, slot] + got[d, 32 * s:32 * s + 32, :].astype(F32)
        return carry

    lax.fori_loop(0, NDEV, add, 0, unroll=4)
    near_copy.wait()

    def item(g, c):
        span = pl.ds((g * NC + c) * 4, 4)
        return (glued[0, span] + glued[1, span]).reshape(NIF, PTS).astype(BF)

    def finish(g, c, n):
        tiles = [item(g, c + i) for i in range(n)]
        added = dot(link[g], tiles[0] if n == 1 else jnp.concatenate(tiles, axis=1))
        for i in range(n):
            at = g * NC + c + i
            out[at, 0:NIF] = (near[at] + added[:, i * PTS:(i + 1) * PTS]).astype(BF)

    def finish_pair(g, i, carry):
        finish(g, 2 * i, 2)
        return carry

    stores = []
    for g in range(2):
        lax.fori_loop(0, 9, functools.partial(finish_pair, g), 0, unroll=3)
        finish(g, 18, 1)
        block = pl.ds(g * NC, NC)
        fars[g].wait()
        stores.append(pltpu.make_async_copy(out.at[block], out_h.at[block], sems.at[5 + g]))
        stores[g].start()
    for store in stores:
        store.wait()


def body(modal, stiffness, mass, freq, coupling, route, target, contact_dof, evaluator, preload):
    slope_table, proj_table = fourier_tables()
    vmem = pl.BlockSpec(memory_space=pltpu.VMEM)
    anywhere = pl.BlockSpec(memory_space=pl.ANY)
    dma = pltpu.SemaphoreType.DMA
    part_f, part_b, got, got_tags = pl.pallas_call(
        main_kernel,
        out_shape=(
            jax.ShapeDtypeStruct((2 * NC, NIF, PTS), F32),
            jax.ShapeDtypeStruct((2 * NC, ND - NIF, PTS), BF),
            jax.ShapeDtypeStruct((NDEV, 64, PTS), BF),
            jax.ShapeDtypeStruct((NDEV, 1, 128), jnp.int32),
        ),
        in_specs=[anywhere] * 3 + [vmem] * 8,
        out_specs=(anywhere,) * 4,
        scratch_shapes=[
            pltpu.VMEM((2 * NC, 4, 32, PTS), BF),
            pltpu.VMEM((2 * NC, 12, 32, PTS), BF),
            pltpu.VMEM((2, ND, ND), BF),
            pltpu.VMEM((2, ND, ND), BF),
            pltpu.VMEM((NDEV, 128), jnp.int32),
            pltpu.SMEM((NDEV, 128), jnp.int32),
            pltpu.VMEM((NDEV, 1, 128), jnp.int32),
            pltpu.VMEM((NDEV, 64, PTS), BF),
            pltpu.VMEM((2, 4, 2, 20, 16, PTS), BF),
            pltpu.VMEM((2, 4, 2, 20, 16, PTS), BF),
            pltpu.VMEM((2, 4, 10, 16, PTS), BF),
            pltpu.VMEM((2, 4, 10, 16, PTS), BF),
            pltpu.VMEM((NZ, 4, 16, PTS), BF),
            pltpu.VMEM((NZ, 4, 16, PTS), BF),
            pltpu.VMEM((NZ, 4, 16, PTS), BF),
            pltpu.VMEM((2, 4, 10, 16, PTS), BF),
            pltpu.VMEM((2, 4, 2, 20, 16, PTS), BF),
            pltpu.VMEM((NC, 2 * ROWS, PTS), F32),
            pltpu.VMEM((NC, 2 * ROWS, PTS), F32),
            pltpu.VMEM((NC, 2 * ROWS, PTS), BF),
            pltpu.VMEM((2 * NC, ND, PTS), F32),
            pltpu.VMEM((2, 2 * ND, ND), BF),
            pltpu.VMEM((2, ND, 2 * ROWS), BF),
            pltpu.VMEM((2 * NC, NIF, PTS), F32),
            pltpu.VMEM((2 * NC, ND - NIF, PTS), BF),
            dma((9,)), dma, dma, dma, dma, dma((6,)), dma((6,)),
        ],
        compiler_params=pltpu.CompilerParams(
            collective_id=1, has_side_effects=True, vmem_limit_bytes=58 << 20
        ),
    )(modal.reshape(2 * NC, 16, 32, PTS), stiffness[0], mass[0], freq.reshape(1, PTS),
      preload, evaluator.reshape(1, ROWS), contact_dof, route.reshape(1, TILES), target,
      jnp.asarray(slope_table), jnp.asarray(proj_table))

    out = pl.pallas_call(
        last_kernel,
        out_shape=jax.ShapeDtypeStruct((2 * NC, ND, PTS), BF),
        in_specs=[anywhere] * 4 + [vmem],
        out_specs=anywhere,
        scratch_shapes=[
            pltpu.VMEM((NDEV, 64, PTS), BF),
            pltpu.SMEM((NDEV, 1, 128), jnp.int32),
            pltpu.VMEM((2 * NC, NIF, PTS), F32),
            pltpu.VMEM((2 * NC, ND, PTS), BF),
            pltpu.VMEM((2, TILES + 1, 32, PTS), F32),
            pltpu.VMEM((2, NIF, NIF), BF),
            dma((7,)),
        ],
        compiler_params=pltpu.CompilerParams(vmem_limit_bytes=58 << 20),
    )(got, got_tags, part_f, part_b, coupling[0])
    return out.reshape(1, 2, NC, ND, PTS)


def solution(mesh):
    placed = (
        P("section", "diam", None, None, None),
        P("section", "diam", None, None),
        P("section", "diam", None, None),
        P(),
        P("section", "diam", None, None, None),
        P("section", "diam", None),
        P("section", "diam"),
        P("section", "diam"),
        P("section", "diam", None),
        P("section", "diam"),
    )
    return jax.shard_map(
        body,
        mesh=mesh,
        in_specs=placed,
        out_specs=P("section", "diam", None, None, None),
        check_vma=False,
    )
```

```python
import functools
import math

import jax
import jax.numpy as jnp
import ml_dtypes
import numpy as np
from jax import lax
from jax.experimental import pallas as pl
from jax.experimental.pallas import tpu as pltpu
from jax.sharding import PartitionSpec as P

HARM = 9
NC = 19
ND = 512
NIF = 128
NT = 128
PTS = 128
NX, NZ, NY = 4, 8, 4
NDEV = 128
TILES = 152
ROWS = 128
STIFF = 0.3
FRICTION = 0.6
MESH = pl.DeviceIdType.MESH
BF = jnp.bfloat16
F32 = jnp.float32


def high_low(table):
    high = table.astype(ml_dtypes.bfloat16)
    low = (table - high.astype(np.float64)).astype(ml_dtypes.bfloat16)
    return high, low


def fourier_tables():
    comp = np.arange(NC)
    order = np.where(comp <= HARM, comp, comp - HARM).astype(np.float64)
    phase = order[:, None] * (np.arange(NT) * (2.0 * math.pi / NT))[None, :]
    sine = (comp > HARM)[:, None]
    slope = np.where(sine, order[:, None] * np.cos(phase), -order[:, None] * np.sin(phase))
    shape = np.where(sine, np.sin(phase), np.cos(phase))
    weight = np.where(comp == 0, 1.0 / NT, 2.0 / NT)
    eye = np.eye(8)
    s_hi, s_lo = high_low(slope[1:].T)
    p_hi, p_lo = high_low(shape * weight[:, None])
    spread = lambda t: np.kron(t.astype(np.float64), eye).astype(ml_dtypes.bfloat16)
    slope_table = np.concatenate([spread(s_hi), spread(s_lo)], axis=1)
    proj_table = np.concatenate([spread(p_hi), spread(p_lo)], axis=0)
    return slope_table, proj_table


def dot(a, b):
    return jnp.dot(a, b, preferred_element_type=F32)


def main_kernel(
    modal_h, stiff_h, mass_h, freq, pre_ref, eval_ref, dof_ref, route_ref, target_ref,
    slope_t, proj_t,
    part_f, part_b, got, got_tags,
    edge, inner, stiff, mass, source, source_s, tags, packed,
    psend, rx, ysend, ry, zsend, rz, agz, agy, agx,
    pay, harm, force, resid, stm, scat, near, far,
    relay, relay_tags,
    l_sem, s_send, s_recv, t_send, t_recv, r_send, r_recv, z_send, z_recv, zt_send, zt_recv,
):
    sec = lax.axis_index("section")
    me = lax.axis_index("diam")
    other = 1 - sec
    x = me // (NZ * NY)
    z = lax.rem(me // NY, NZ)
    y = lax.rem(me, NY)

    def at(px, pz, py):
        return (px * NZ + pz) * NY + py

    def x_peer(k):
        return lax.rem(x + k, NX)

    def y_peer(k):
        return lax.rem(y + k, NY)

    def z_peer(k):
        return lax.rem(z + k, NZ)

    loads = [
        pltpu.make_async_copy(modal_h.at[:, 0:4], edge, l_sem.at[0]),
        pltpu.make_async_copy(modal_h.at[:, 4:16], inner, l_sem.at[1]),
        pltpu.make_async_copy(stiff_h, stiff, l_sem.at[2]),
        pltpu.make_async_copy(mass_h, mass, l_sem.at[3]),
    ]
    for load in loads:
        load.start()

    barrier = pltpu.get_barrier_semaphore()

    for k in range(NX * NY):
        there = at(x_peer(k // NY), z, y_peer(k % NY))
        pl.semaphore_signal(barrier, inc=1, device_id=(other, there), device_id_type=MESH)
    for k in range(1, NX):
        pl.semaphore_signal(barrier, inc=1, device_id=(sec, at(x_peer(k), z, y)), device_id_type=MESH)
    for k in range(1, NY):
        pl.semaphore_signal(barrier, inc=1, device_id=(sec, at(x, z, y_peer(k))), device_id_type=MESH)
    for k in range(1, NZ):
        pl.semaphore_signal(barrier, inc=1, device_id=(sec, at(x, z_peer(k), y)), device_id_type=MESH)

    spot = lax.broadcasted_iota(jnp.int32, (NDEV, TILES), 1)
    row = lax.broadcasted_iota(jnp.int32, (NDEV, TILES), 0)
    inside = jnp.bitwise_and(row, 15)
    owner = (
        jnp.right_shift(inside, 2) * (NZ * NY) + jnp.right_shift(row, 4) * NY
        + jnp.bitwise_and(inside, 3)
    )
    named = route_ref[...] == owner
    key = (spot * 256 + target_ref[...])
    first = jnp.min(jnp.where(named, key, 1 << 20), axis=1, keepdims=True)
    final = jnp.max(jnp.where(named, key, -1), axis=1, keepdims=True)
    none = jnp.full_like(first, TILES)
    one_key = jnp.where(first < (1 << 20), first, none)
    two_key = jnp.where((final >= 0) & (final != first), final, none)
    lane = lax.broadcasted_iota(jnp.int32, (NDEV, 128), 1)
    keys = jnp.where(lane < 64, one_key, two_key)
    source[...] = jnp.right_shift(keys, 8)
    tags[...] = jnp.bitwise_and(keys, 255).reshape(NDEV, 1, 128)
    listing = pltpu.make_async_copy(source, source_s, l_sem.at[4])
    listing.start()

    loads[0].wait()
    listing.wait()

    def tile(t):
        return edge[jnp.right_shift(t, 2), jnp.bitwise_and(t, 3)]

    def pack(d, carry):
        packed[d, 0:32, :] = tile(source_s[d, 0])
        packed[d, 32:64, :] = tile(source_s[d, 64])
        return carry

    lax.fori_loop(0, NDEV, pack, 0)
    pl.semaphore_wait(barrier, NX * NY + NX + NY + NZ - 3)


    def along(k):
        to = z_peer(k)
        chunk = pl.ds(16 * to, 16)
        there = (sec, at(x, to, y))
        pltpu.make_async_remote_copy(
            src_ref=tags.at[chunk], dst_ref=relay_tags.at[z], send_sem=zt_send,
            recv_sem=zt_recv.at[k], device_id=there, device_id_type=MESH,
        ).start()
        pltpu.make_async_remote_copy(
            src_ref=packed.at[chunk], dst_ref=relay.at[z], send_sem=z_send,
            recv_sem=z_recv.at[k], device_id=there, device_id_type=MESH,
        ).start()

    along(1)
    along(7)

    pre_row = pre_ref[...].astype(F32)
    eval_row = eval_ref[...].astype(F32)
    dof_row = dof_ref[...].astype(F32)
    dof_col = jnp.transpose(jnp.broadcast_to(dof_row, (ROWS, ROWS)))
    lane512 = lax.broadcasted_iota(jnp.int32, (ROWS, ND), 1).astype(F32)
    sub512 = lax.broadcasted_iota(jnp.int32, (ND, ROWS), 0).astype(F32)
    picks = []
    for g in range(2):
        halves = []
        for a in range(2):
            here = dof_col[:, 0:1] * 2.0 + (a - g * ND)
            halves.append(jnp.where(lane512 == here, 1.0, 0.0).astype(BF))
            there = dof_row * 2.0 + (a - g * ND)
            scat[g, :, a * ROWS:(a + 1) * ROWS] = jnp.where(sub512 == there, 1.0, 0.0).astype(BF)
        picks.append(jnp.concatenate(halves, axis=0))
    sub128 = lax.broadcasted_iota(jnp.int32, (ROWS, ROWS), 0).astype(F32)
    weights32 = jnp.where(sub128 == eval_row, pre_row, 0.0)
    weights = weights32.astype(BF)
    load = jnp.broadcast_to(jnp.sum(weights32, axis=1, keepdims=True), (NDEV, PTS))
    load_hi = load.astype(BF)
    psend[1, :, :, 18] = load_hi.reshape(4, 2, 16, PTS)
    psend[1, :, :, 19] = (load - load_hi.astype(F32)).astype(BF).reshape(4, 2, 16, PTS)
    loads[1].wait()

    def comps(g, c, n):
        tiles = []
        for i in range(n):
            item = g * NC + c + i
            parts = [edge[item].reshape(NIF, PTS), inner[item].reshape(ND - NIF, PTS)]
            tiles.append(jnp.concatenate(parts, axis=0))
        return tiles[0] if n == 1 else jnp.concatenate(tiles, axis=1)

    def gather(c, n, half):
        got_rows = dot(picks[0], comps(0, c, n)) + dot(picks[1], comps(1, c, n))
        narrow = got_rows.astype(BF)
        for i in range(n):
            pay[c + i] = got_rows[:, i * PTS:(i + 1) * PTS]
        for a in range(2):
            summed = dot(weights, narrow[a * ROWS:(a + 1) * ROWS]).astype(BF)
            for i in range(n):
                part = summed[:, i * PTS:(i + 1) * PTS].reshape(4, 2, 16, PTS)
                psend[half, :, :, (c + i) * 2 + a - 20 * half] = part

    def gather_pair(half, i, carry):
        gather(2 * i, 2, half)
        return carry

    lax.fori_loop(0, 5, functools.partial(gather_pair, 0), 0)
    lax.fori_loop(5, 9, functools.partial(gather_pair, 1), 0)
    gather(18, 1, 1)

    def push(src, dst, step, device):
        pltpu.make_async_remote_copy(
            src_ref=src, dst_ref=dst, send_sem=r_send.at[step], recv_sem=r_recv.at[step],
            device_id=device, device_id_type=MESH,
        ).start()

    def arrived(ref, step):
        pltpu.make_async_copy(ref, ref, r_recv.at[step]).wait()

    def left(ref, step):
        pltpu.make_async_copy(ref, ref, r_send.at[step]).wait()

    mine = ((x, y), (y, x))
    peers = ((x_peer, y_peer), (y_peer, x_peer))

    def device(half, turn, k):
        if half == turn:
            return sec, at(x_peer(k), z, y)
        return sec, at(x, z, y_peer(k))

    for k in range(1, 4):
        for half in range(2):
            push(psend.at[half, peers[half][0](k)], rx.at[half, mine[half][0]], 0, device(half, 0, k))

    def across(k):
        origin = lax.rem(z + NZ - k, NZ)
        if k:
            pltpu.make_async_copy(relay_tags.at[0], relay_tags.at[0], zt_recv.at[k]).wait()
            pltpu.make_async_copy(relay.at[0], relay.at[0], z_recv.at[k]).wait()
        slot = at(x, origin, y)

        def one(j, carry):
            px, py = lax.rem(x + j // NY, NX), lax.rem(y + lax.rem(j, NY), NY)
            d = at(px, z, py)
            spot = px * NY + py
            if k:
                tag, tile = relay_tags.at[origin, spot], relay.at[origin, spot]
            else:
                tag, tile = tags.at[16 * z + spot], packed.at[16 * z + spot]
            pltpu.make_async_remote_copy(
                src_ref=tag, dst_ref=got_tags.at[slot], send_sem=t_send, recv_sem=t_recv,
                device_id=(other, d), device_id_type=MESH,
            ).start()
            pltpu.make_async_remote_copy(
                src_ref=tile, dst_ref=got.at[slot], send_sem=s_send, recv_sem=s_recv,
                device_id=(other, d), device_id_type=MESH,
            ).start()
            return carry

        lax.fori_loop(0, NX * NY, one, 0)

    along(2)
    along(6)
    loads[2].wait()
    loads[3].wait()
    for g in range(2):
        stm[g, 0:ND] = jnp.transpose(stiff[g])
        stm[g, ND:2 * ND] = jnp.transpose(mass[g])

    soft = 0.01 / (freq[...] * freq[...])

    def contact(b, carry):
        low = pl.multiple_of(b * 8, 8)
        sides = []
        for a in range(2):
            lines = [pay[c, pl.ds(a * ROWS + low, 8), :] for c in range(1, NC)]
            sides.append(jnp.concatenate(lines, axis=0))
        values = jnp.concatenate(sides, axis=1).astype(BF)
        speed = dot(slope_t[...], jnp.concatenate([values, values], axis=0))
        one, two = speed[:, 0:PTS], speed[:, PTS:2 * PTS]
        inverse = lax.rsqrt(one * one + two * two + soft)
        slide = jnp.concatenate([(one * inverse).astype(BF), (two * inverse).astype(BF)], axis=1)
        both = dot(proj_t[...], slide)
        total = both[0:8 * NC] + both[8 * NC:16 * NC]
        for c in range(NC):
            for a in range(2):
                harm[c, pl.ds(a * ROWS + low, 8), :] = total[8 * c:8 * c + 8, a * PTS:(a + 1) * PTS]
        return carry

    lax.fori_loop(0, 8, contact, 0, unroll=2)

    def split(total):
        high = total.astype(BF)
        return high, (total - high.astype(F32)).astype(BF)

    arrived(rx.at[:, 0:3], 0)
    for half in range(2):
        whole = psend[half, mine[half][0]].astype(F32)
        for k in range(1, 4):
            whole = whole + rx[half, peers[half][0](k)].astype(F32)
        for g in range(2):
            for part in range(2):
                ysend[half, 2 * g + part] = whole[g, 10 * part:10 * part + 10].astype(BF)
        if half == 1:
            high, low = split(whole[:, 18] + whole[:, 19])
            for g in range(2):
                ysend[1, 2 * g + 1, 8] = high[g]
                ysend[1, 2 * g + 1, 9] = low[g]
    for k in range(1, 4):
        for half in range(2):
            push(ysend.at[half, peers[half][1](k)], ry.at[half, mine[half][1]], 1, device(half, 1, k))
    lax.fori_loop(8, 12, contact, 0, unroll=2)

    odd = lax.rem(x, 2) == 1
    arrived(ry.at[:, 0:3], 1)
    zsend[5:8] = jnp.zeros((3, 4, 16, PTS), BF)
    for half in range(2):
        whole = ysend[half, mine[half][1]].astype(F32)
        for k in range(1, 4):
            whole = whole + ry[half, peers[half][1](k)].astype(F32)
        for part in range(5):
            zsend[part, 2 * half:2 * half + 2] = whole[2 * part:2 * part + 2].astype(BF)
        if half == 1:
            high, low = split(whole[8] + whole[9])
            zsend[4, 2] = jnp.where(odd, high.astype(F32), whole[8]).astype(BF)
            zsend[4, 3] = jnp.where(odd, low.astype(F32), whole[9]).astype(BF)
    for k in range(1, NZ):
        push(zsend.at[z_peer(k)], rz.at[z], 2, (sec, at(x, z_peer(k), y)))
    across(0)
    across(1)
    across(7)
    lax.fori_loop(12, 16, contact, 0, unroll=2)

    def balance(g, c, n):
        both = dot(stm[g], comps(g, c, n))
        for i in range(n):
            h = jnp.where(c + i <= HARM, c + i, c + i - HARM)
            scaled = jnp.asarray(h, jnp.int32).astype(F32) * freq[...]
            lanes = slice(i * PTS, (i + 1) * PTS)
            resid[g * NC + c + i] = both[0:ND, lanes] - (scaled * scaled) * both[ND:2 * ND, lanes]

    def balance_pair(g, i, carry):
        balance(g, 2 * i, 2)
        return carry

    arrived(rz.at[0:7], 2)
    whole = zsend[z].astype(F32)
    for k in range(1, NZ):
        whole = whole + rz[z_peer(k)].astype(F32)
    high, low = split(whole[2] + whole[3])
    here = jnp.logical_and(odd, z == 4)
    agz[z, 0:2] = whole[0:2].astype(BF)
    agz[z, 2] = jnp.where(here, high.astype(F32), whole[2]).astype(BF)
    agz[z, 3] = jnp.where(here, low.astype(F32), whole[3]).astype(BF)
    for k in range(1, NZ):
        push(agz.at[z], agz.at[z], 3, (sec, at(x, z_peer(k), y)))
    along(3)
    along(5)
    along(4)
    across(2)
    across(6)
    lax.fori_loop(0, 5, functools.partial(balance_pair, 0), 0)

    arrived(agz.at[0:7], 3)
    for half in range(2):
        agy[half, mine[half][1]] = agz[0:5, 2 * half:2 * half + 2].reshape(10, 16, PTS)
        for k in range(1, 4):
            slot = agy.at[half, mine[half][1]]
            push(slot, slot, 4, device(half, 1, k))
    lax.fori_loop(5, 9, functools.partial(balance_pair, 0), 0)
    balance(0, 18, 1)

    arrived(agy.at[:, 0:3], 4)
    for half in range(2):
        agx[half, mine[half][0]] = agy[half].reshape(2, 20, 16, PTS)
        for k in range(1, 4):
            slot = agx.at[half, mine[half][0]]
            push(slot, slot, 5, device(half, 0, k))
    lax.fori_loop(0, 9, functools.partial(balance_pair, 1), 0, unroll=3)
    balance(1, 18, 1)
    arrived(agx.at[:, 0:3], 5)

    lane128 = lax.broadcasted_iota(jnp.int32, (ROWS, ROWS), 1).astype(F32)
    eval_col = jnp.transpose(jnp.broadcast_to(eval_row, (ROWS, ROWS)))
    pre_col = jnp.transpose(jnp.broadcast_to(pre_row, (ROWS, ROWS)))
    choose = jnp.where(lane128 == eval_col, 1.0, 0.0).astype(BF)

    def joints(half, k):
        return agx[half, :, :, k].reshape(NDEV, PTS)

    loaded = dot(choose, jnp.concatenate([joints(1, 18), joints(1, 19)], axis=1))
    per_load = 1.0 / (loaded[:, 0:PTS] + loaded[:, PTS:2 * PTS])
    pressed = pre_col * (FRICTION * ROWS) * per_load

    def forces(half, c, carry):
        k = 2 * c - 20 * half
        mean = dot(choose, jnp.concatenate([joints(half, k), joints(half, k + 1)], axis=1))
        for a in range(2):
            rows = slice(a * ROWS, (a + 1) * ROWS)
            away = pay[c, rows, :] - mean[:, a * PTS:(a + 1) * PTS] * per_load
            force[c, rows, :] = (STIFF * away + pressed * harm[c, rows, :]).astype(BF)
        return carry

    lax.fori_loop(0, 10, functools.partial(forces, 0), 0, unroll=2)
    lax.fori_loop(10, NC, functools.partial(forces, 1), 0, unroll=3)

    def finish(g, c, n):
        lines = [force[c + i] for i in range(n)]
        added = dot(scat[g], lines[0] if n == 1 else jnp.concatenate(lines, axis=1))
        for i in range(n):
            item = g * NC + c + i
            value = resid[item] + added[:, i * PTS:(i + 1) * PTS]
            near[item] = value[0:NIF]
            far[item] = value[NIF:ND].astype(BF)

    def finish_pair(g, i, carry):
        finish(g, 2 * i, 2)
        return carry

    stores = []
    for g in range(2):
        lax.fori_loop(0, 9, functools.partial(finish_pair, g), 0, unroll=3)
        finish(g, 18, 1)
        block = pl.ds(g * NC, NC)
        stores.append(pltpu.make_async_copy(far.at[block], part_b.at[block], l_sem.at[5 + g]))
        stores.append(pltpu.make_async_copy(near.at[block], part_f.at[block], l_sem.at[7 + g]))
        stores[-2].start()
        stores[-1].start()

    across(3)
    across(5)
    across(4)
    left(rx.at[:, 0:3], 0)
    left(ry.at[:, 0:3], 1)
    left(rz.at[0:7], 2)
    left(agz.at[0:7], 3)
    left(agy.at[:, 0:3], 4)
    left(agx.at[:, 0:3], 5)
    for store in stores:
        store.wait()
    pltpu.make_async_copy(relay.at[0:7], relay.at[0:7], z_send).wait()
    pltpu.make_async_copy(relay_tags.at[0:7], relay_tags.at[0:7], zt_send).wait()
    pltpu.make_async_copy(packed, packed, s_send).wait()
    pltpu.make_async_copy(tags, tags, t_send).wait()
    pltpu.make_async_copy(got_tags, got_tags, t_recv).wait()
    pltpu.make_async_copy(got, got, s_recv).wait()


def last_kernel(
    got_h, tags_h, part_f, part_b, coupling, out_h,
    got, tags, near, out, glued, link, sems,
):
    tag_copy = pltpu.make_async_copy(tags_h, tags, sems.at[0])
    got_copy = pltpu.make_async_copy(got_h, got, sems.at[1])
    near_copy = pltpu.make_async_copy(part_f, near, sems.at[2])
    tag_copy.start()
    got_copy.start()
    near_copy.start()
    fars = []
    for g in range(2):
        block = pl.ds(g * NC, NC)
        fars.append(pltpu.make_async_copy(part_b.at[block], out.at[block, NIF:ND], sems.at[3 + g]))
        fars[g].start()
    glued[...] = jnp.zeros_like(glued)
    link[...] = jnp.zeros_like(link)
    for g in range(2):
        for q in range(4):
            span = slice(32 * q, 32 * q + 32)
            link[g, span, span] = jnp.transpose(coupling[g, q].astype(F32)).astype(BF)
    tag_copy.wait()
    got_copy.wait()

    def add(d, carry):
        for s in range(2):
            slot = tags[d, 0, 64 * s]
            glued[s, slot] = glued[s, slot] + got[d, 32 * s:32 * s + 32, :].astype(F32)
        return carry

    lax.fori_loop(0, NDEV, add, 0, unroll=4)
    near_copy.wait()

    def item(g, c):
        span = pl.ds((g * NC + c) * 4, 4)
        return (glued[0, span] + glued[1, span]).reshape(NIF, PTS).astype(BF)

    def finish(g, c, n):
        tiles = [item(g, c + i) for i in range(n)]
        added = dot(link[g], tiles[0] if n == 1 else jnp.concatenate(tiles, axis=1))
        for i in range(n):
            at = g * NC + c + i
            out[at, 0:NIF] = (near[at] + added[:, i * PTS:(i + 1) * PTS]).astype(BF)

    def finish_pair(g, i, carry):
        finish(g, 2 * i, 2)
        return carry

    stores = []
    for g in range(2):
        lax.fori_loop(0, 9, functools.partial(finish_pair, g), 0, unroll=3)
        finish(g, 18, 1)
        block = pl.ds(g * NC, NC)
        fars[g].wait()
        stores.append(pltpu.make_async_copy(out.at[block], out_h.at[block], sems.at[5 + g]))
        stores[g].start()
    for store in stores:
        store.wait()


def body(modal, stiffness, mass, freq, coupling, route, target, contact_dof, evaluator, preload):
    slope_table, proj_table = fourier_tables()
    vmem = pl.BlockSpec(memory_space=pltpu.VMEM)
    anywhere = pl.BlockSpec(memory_space=pl.ANY)
    dma = pltpu.SemaphoreType.DMA
    part_f, part_b, got, got_tags = pl.pallas_call(
        main_kernel,
        out_shape=(
            jax.ShapeDtypeStruct((2 * NC, NIF, PTS), F32),
            jax.ShapeDtypeStruct((2 * NC, ND - NIF, PTS), BF),
            jax.ShapeDtypeStruct((NDEV, 64, PTS), BF),
            jax.ShapeDtypeStruct((NDEV, 1, 128), jnp.int32),
        ),
        in_specs=[anywhere] * 3 + [vmem] * 8,
        out_specs=(anywhere,) * 4,
        scratch_shapes=[
            pltpu.VMEM((2 * NC, 4, 32, PTS), BF),
            pltpu.VMEM((2 * NC, 12, 32, PTS), BF),
            pltpu.VMEM((2, ND, ND), BF),
            pltpu.VMEM((2, ND, ND), BF),
            pltpu.VMEM((NDEV, 128), jnp.int32),
            pltpu.SMEM((NDEV, 128), jnp.int32),
            pltpu.VMEM((NDEV, 1, 128), jnp.int32),
            pltpu.VMEM((NDEV, 64, PTS), BF),
            pltpu.VMEM((2, 4, 2, 20, 16, PTS), BF),
            pltpu.VMEM((2, 4, 2, 20, 16, PTS), BF),
            pltpu.VMEM((2, 4, 10, 16, PTS), BF),
            pltpu.VMEM((2, 4, 10, 16, PTS), BF),
            pltpu.VMEM((NZ, 4, 16, PTS), BF),
            pltpu.VMEM((NZ, 4, 16, PTS), BF),
            pltpu.VMEM((NZ, 4, 16, PTS), BF),
            pltpu.VMEM((2, 4, 10, 16, PTS), BF),
            pltpu.VMEM((2, 4, 2, 20, 16, PTS), BF),
            pltpu.VMEM((NC, 2 * ROWS, PTS), F32),
            pltpu.VMEM((NC, 2 * ROWS, PTS), F32),
            pltpu.VMEM((NC, 2 * ROWS, PTS), BF),
            pltpu.VMEM((2 * NC, ND, PTS), F32),
            pltpu.VMEM((2, 2 * ND, ND), BF),
            pltpu.VMEM((2, ND, 2 * ROWS), BF),
            pltpu.VMEM((2 * NC, NIF, PTS), F32),
            pltpu.VMEM((2 * NC, ND - NIF, PTS), BF),
            pltpu.VMEM((NZ, 16, 64, PTS), BF),
            pltpu.VMEM((NZ, 16, 1, 128), jnp.int32),
            dma((9,)), dma, dma, dma, dma, dma((6,)), dma((6,)), dma, dma((NZ,)), dma, dma((NZ,)),
        ],
        compiler_params=pltpu.CompilerParams(
            collective_id=1, has_side_effects=True, vmem_limit_bytes=58 << 20
        ),
    )(modal.reshape(2 * NC, 16, 32, PTS), stiffness[0], mass[0], freq.reshape(1, PTS),
      preload, evaluator.reshape(1, ROWS), contact_dof, route.reshape(1, TILES), target,
      jnp.asarray(slope_table), jnp.asarray(proj_table))

    out = pl.pallas_call(
        last_kernel,
        out_shape=jax.ShapeDtypeStruct((2 * NC, ND, PTS), BF),
        in_specs=[anywhere] * 4 + [vmem],
        out_specs=anywhere,
        scratch_shapes=[
            pltpu.VMEM((NDEV, 64, PTS), BF),
            pltpu.SMEM((NDEV, 1, 128), jnp.int32),
            pltpu.VMEM((2 * NC, NIF, PTS), F32),
            pltpu.VMEM((2 * NC, ND, PTS), BF),
            pltpu.VMEM((2, TILES + 1, 32, PTS), F32),
            pltpu.VMEM((2, NIF, NIF), BF),
            dma((7,)),
        ],
        compiler_params=pltpu.CompilerParams(vmem_limit_bytes=58 << 20),
    )(got, got_tags, part_f, part_b, coupling[0])
    return out.reshape(1, 2, NC, ND, PTS)


def solution(mesh):
    placed = (
        P("section", "diam", None, None, None),
        P("section", "diam", None, None),
        P("section", "diam", None, None),
        P(),
        P("section", "diam", None, None, None),
        P("section", "diam", None),
        P("section", "diam"),
        P("section", "diam"),
        P("section", "diam", None),
        P("section", "diam"),
    )
    return jax.shard_map(
        body,
        mesh=mesh,
        in_specs=placed,
        out_specs=P("section", "diam", None, None, None),
        check_vma=False,
    )
```

```python
import functools
import math

import jax
import jax.numpy as jnp
import ml_dtypes
import numpy as np
from jax import lax
from jax.experimental import pallas as pl
from jax.experimental.pallas import tpu as pltpu
from jax.sharding import PartitionSpec as P

HARM = 9
NC = 19
ND = 512
NIF = 128
NT = 128
PTS = 128
NX, NZ, NY = 4, 8, 4
NDEV = 128
TILES = 152
ROWS = 128
STIFF = 0.3
FRICTION = 0.6
MESH = pl.DeviceIdType.MESH
BF = jnp.bfloat16
F32 = jnp.float32


def high_low(table):
    high = table.astype(ml_dtypes.bfloat16)
    low = (table - high.astype(np.float64)).astype(ml_dtypes.bfloat16)
    return high, low


def fourier_tables():
    comp = np.arange(NC)
    order = np.where(comp <= HARM, comp, comp - HARM).astype(np.float64)
    phase = order[:, None] * (np.arange(NT) * (2.0 * math.pi / NT))[None, :]
    sine = (comp > HARM)[:, None]
    slope = np.where(sine, order[:, None] * np.cos(phase), -order[:, None] * np.sin(phase))
    shape = np.where(sine, np.sin(phase), np.cos(phase))
    weight = np.where(comp == 0, 1.0 / NT, 2.0 / NT)
    eye = np.eye(8)
    s_hi, s_lo = high_low(slope[1:].T)
    p_hi, p_lo = high_low(shape * weight[:, None])
    spread = lambda t: np.kron(t.astype(np.float64), eye).astype(ml_dtypes.bfloat16)
    slope_table = np.concatenate([spread(s_hi), spread(s_lo)], axis=1)
    proj_table = np.concatenate([spread(p_hi), spread(p_lo)], axis=0)
    return slope_table, proj_table


def dot(a, b):
    return jnp.dot(a, b, preferred_element_type=F32)


def main_kernel(
    modal_h, stiff_h, mass_h, freq, pre_ref, eval_ref, dof_ref, route_ref, target_ref,
    slope_t, proj_t,
    part_f, part_b, got, got_tags,
    edge, inner, stiff, mass, source, source_s, tags, packed,
    psend, rx, ysend, ry, zsend, rz, agz, agy, agx,
    pay, harm, force, resid, stm, scat, near, far,
    relay, relay_tags,
    l_sem, s_send, s_recv, t_send, t_recv, r_send, r_recv, z_send, z_recv, zt_send, zt_recv,
):
    sec = lax.axis_index("section")
    me = lax.axis_index("diam")
    other = 1 - sec
    x = me // (NZ * NY)
    z = lax.rem(me // NY, NZ)
    y = lax.rem(me, NY)

    def at(px, pz, py):
        return (px * NZ + pz) * NY + py

    def x_peer(k):
        return lax.rem(x + k, NX)

    def y_peer(k):
        return lax.rem(y + k, NY)

    def z_peer(k):
        return lax.rem(z + k, NZ)

    loads = [
        pltpu.make_async_copy(modal_h.at[:, 0:4], edge, l_sem.at[0]),
        pltpu.make_async_copy(modal_h.at[:, 4:16], inner, l_sem.at[1]),
        pltpu.make_async_copy(stiff_h, stiff, l_sem.at[2]),
        pltpu.make_async_copy(mass_h, mass, l_sem.at[3]),
    ]
    for load in loads:
        load.start()

    barrier = pltpu.get_barrier_semaphore()

    for k in range(NX * NY):
        there = at(x_peer(k // NY), z, y_peer(k % NY))
        pl.semaphore_signal(barrier, inc=1, device_id=(other, there), device_id_type=MESH)
    for k in range(1, NX):
        pl.semaphore_signal(barrier, inc=1, device_id=(sec, at(x_peer(k), z, y)), device_id_type=MESH)
    for k in range(1, NY):
        pl.semaphore_signal(barrier, inc=1, device_id=(sec, at(x, z, y_peer(k))), device_id_type=MESH)
    for k in range(1, NZ):
        pl.semaphore_signal(barrier, inc=1, device_id=(sec, at(x, z_peer(k), y)), device_id_type=MESH)

    spot = lax.broadcasted_iota(jnp.int32, (NDEV, TILES), 1)
    row = lax.broadcasted_iota(jnp.int32, (NDEV, TILES), 0)
    inside = jnp.bitwise_and(row, 15)
    owner = (
        jnp.right_shift(inside, 2) * (NZ * NY) + jnp.right_shift(row, 4) * NY
        + jnp.bitwise_and(inside, 3)
    )
    named = route_ref[...] == owner
    key = (spot * 256 + target_ref[...])
    first = jnp.min(jnp.where(named, key, 1 << 20), axis=1, keepdims=True)
    final = jnp.max(jnp.where(named, key, -1), axis=1, keepdims=True)
    none = jnp.full_like(first, TILES)
    one_key = jnp.where(first < (1 << 20), first, none)
    two_key = jnp.where((final >= 0) & (final != first), final, none)
    lane = lax.broadcasted_iota(jnp.int32, (NDEV, 128), 1)
    keys = jnp.where(lane < 64, one_key, two_key)
    source[...] = jnp.right_shift(keys, 8)
    tags[...] = jnp.bitwise_and(keys, 255).reshape(NDEV, 1, 128)
    listing = pltpu.make_async_copy(source, source_s, l_sem.at[4])
    listing.start()

    loads[0].wait()
    listing.wait()

    def tile(t):
        return edge[jnp.right_shift(t, 2), jnp.bitwise_and(t, 3)]

    def pack(d, carry):
        packed[d, 0:32, :] = tile(source_s[d, 0])
        packed[d, 32:64, :] = tile(source_s[d, 64])
        return carry

    lax.fori_loop(0, NDEV, pack, 0)
    pl.semaphore_wait(barrier, NX * NY + NX + NY + NZ - 3)


    def along(k):
        to = z_peer(k)
        chunk = pl.ds(16 * to, 16)
        there = (sec, at(x, to, y))
        pltpu.make_async_remote_copy(
            src_ref=tags.at[chunk], dst_ref=relay_tags.at[z], send_sem=zt_send,
            recv_sem=zt_recv.at[k], device_id=there, device_id_type=MESH,
        ).start()
        pltpu.make_async_remote_copy(
            src_ref=packed.at[chunk], dst_ref=relay.at[z], send_sem=z_send,
            recv_sem=z_recv.at[k], device_id=there, device_id_type=MESH,
        ).start()

    along(1)
    along(7)

    pre_row = pre_ref[...].astype(F32)
    eval_row = eval_ref[...].astype(F32)
    dof_row = dof_ref[...].astype(F32)
    dof_col = jnp.transpose(jnp.broadcast_to(dof_row, (ROWS, ROWS)))
    lane512 = lax.broadcasted_iota(jnp.int32, (ROWS, ND), 1).astype(F32)
    sub512 = lax.broadcasted_iota(jnp.int32, (ND, ROWS), 0).astype(F32)
    picks = []
    for g in range(2):
        halves = []
        for a in range(2):
            here = dof_col[:, 0:1] * 2.0 + (a - g * ND)
            halves.append(jnp.where(lane512 == here, 1.0, 0.0).astype(BF))
            there = dof_row * 2.0 + (a - g * ND)
            scat[g, :, a * ROWS:(a + 1) * ROWS] = jnp.where(sub512 == there, 1.0, 0.0).astype(BF)
        picks.append(jnp.concatenate(halves, axis=0))
    sub128 = lax.broadcasted_iota(jnp.int32, (ROWS, ROWS), 0).astype(F32)
    weights32 = jnp.where(sub128 == eval_row, pre_row, 0.0)
    weights = weights32.astype(BF)
    load = jnp.broadcast_to(jnp.sum(weights32, axis=1, keepdims=True), (NDEV, PTS))
    load_hi = load.astype(BF)
    psend[1, :, :, 18] = load_hi.reshape(4, 2, 16, PTS)
    psend[1, :, :, 19] = (load - load_hi.astype(F32)).astype(BF).reshape(4, 2, 16, PTS)
    loads[1].wait()

    def comps(g, c, n):
        tiles = []
        for i in range(n):
            item = g * NC + c + i
            parts = [edge[item].reshape(NIF, PTS), inner[item].reshape(ND - NIF, PTS)]
            tiles.append(jnp.concatenate(parts, axis=0))
        return tiles[0] if n == 1 else jnp.concatenate(tiles, axis=1)

    def gather(c, n, half):
        got_rows = dot(picks[0], comps(0, c, n)) + dot(picks[1], comps(1, c, n))
        narrow = got_rows.astype(BF)
        for i in range(n):
            pay[c + i] = got_rows[:, i * PTS:(i + 1) * PTS]
        for a in range(2):
            summed = dot(weights, narrow[a * ROWS:(a + 1) * ROWS]).astype(BF)
            for i in range(n):
                part = summed[:, i * PTS:(i + 1) * PTS].reshape(4, 2, 16, PTS)
                psend[half, :, :, (c + i) * 2 + a - 20 * half] = part

    def gather_pair(half, i, carry):
        gather(2 * i, 2, half)
        return carry

    lax.fori_loop(0, 5, functools.partial(gather_pair, 0), 0)
    lax.fori_loop(5, 9, functools.partial(gather_pair, 1), 0)
    gather(18, 1, 1)

    def push(src, dst, step, device):
        pltpu.make_async_remote_copy(
            src_ref=src, dst_ref=dst, send_sem=r_send.at[step], recv_sem=r_recv.at[step],
            device_id=device, device_id_type=MESH,
        ).start()

    def arrived(ref, step):
        pltpu.make_async_copy(ref, ref, r_recv.at[step]).wait()

    def left(ref, step):
        pltpu.make_async_copy(ref, ref, r_send.at[step]).wait()

    mine = ((x, y), (y, x))
    peers = ((x_peer, y_peer), (y_peer, x_peer))

    def device(half, turn, k):
        if half == turn:
            return sec, at(x_peer(k), z, y)
        return sec, at(x, z, y_peer(k))

    for k in range(1, 4):
        for half in range(2):
            push(psend.at[half, peers[half][0](k)], rx.at[half, mine[half][0]], 0, device(half, 0, k))

    def across(k):
        origin = lax.rem(z + NZ - k, NZ)
        if k:
            pltpu.make_async_copy(relay_tags.at[0], relay_tags.at[0], zt_recv.at[k]).wait()
            pltpu.make_async_copy(relay.at[0], relay.at[0], z_recv.at[k]).wait()
        slot = at(x, origin, y)

        def one(j, carry):
            px, py = lax.rem(x + j // NY, NX), lax.rem(y + lax.rem(j, NY), NY)
            d = at(px, z, py)
            spot = px * NY + py
            if k:
                tag, tile = relay_tags.at[origin, spot], relay.at[origin, spot]
            else:
                tag, tile = tags.at[16 * z + spot], packed.at[16 * z + spot]
            pltpu.make_async_remote_copy(
                src_ref=tag, dst_ref=got_tags.at[slot], send_sem=t_send, recv_sem=t_recv,
                device_id=(other, d), device_id_type=MESH,
            ).start()
            pltpu.make_async_remote_copy(
                src_ref=tile, dst_ref=got.at[slot], send_sem=s_send, recv_sem=s_recv,
                device_id=(other, d), device_id_type=MESH,
            ).start()
            return carry

        lax.fori_loop(0, NX * NY, one, 0)

    along(2)
    along(6)
    loads[2].wait()
    loads[3].wait()
    for g in range(2):
        stm[g, 0:ND] = jnp.transpose(stiff[g])
        stm[g, ND:2 * ND] = jnp.transpose(mass[g])

    soft = 0.01 / (freq[...] * freq[...])

    def contact(b, carry):
        low = pl.multiple_of(b * 8, 8)
        sides = []
        for a in range(2):
            lines = [pay[c, pl.ds(a * ROWS + low, 8), :] for c in range(1, NC)]
            sides.append(jnp.concatenate(lines, axis=0))
        values = jnp.concatenate(sides, axis=1).astype(BF)
        speed = dot(slope_t[...], jnp.concatenate([values, values], axis=0))
        one, two = speed[:, 0:PTS], speed[:, PTS:2 * PTS]
        inverse = lax.rsqrt(one * one + two * two + soft)
        slide = jnp.concatenate([(one * inverse).astype(BF), (two * inverse).astype(BF)], axis=1)
        both = dot(proj_t[...], slide)
        total = both[0:8 * NC] + both[8 * NC:16 * NC]
        for c in range(NC):
            for a in range(2):
                harm[c, pl.ds(a * ROWS + low, 8), :] = total[8 * c:8 * c + 8, a * PTS:(a + 1) * PTS]
        return carry

    lax.fori_loop(0, 8, contact, 0, unroll=2)

    def split(total):
        high = total.astype(BF)
        return high, (total - high.astype(F32)).astype(BF)

    along(4)
    arrived(rx.at[:, 0:3], 0)
    for half in range(2):
        whole = psend[half, mine[half][0]].astype(F32)
        for k in range(1, 4):
            whole = whole + rx[half, peers[half][0](k)].astype(F32)
        for g in range(2):
            for part in range(2):
                ysend[half, 2 * g + part] = whole[g, 10 * part:10 * part + 10].astype(BF)
        if half == 1:
            high, low = split(whole[:, 18] + whole[:, 19])
            for g in range(2):
                ysend[1, 2 * g + 1, 8] = high[g]
                ysend[1, 2 * g + 1, 9] = low[g]
    for k in range(1, 4):
        for half in range(2):
            push(ysend.at[half, peers[half][1](k)], ry.at[half, mine[half][1]], 1, device(half, 1, k))
    lax.fori_loop(8, 12, contact, 0, unroll=2)

    odd = lax.rem(x, 2) == 1
    arrived(ry.at[:, 0:3], 1)
    zsend[5:8] = jnp.zeros((3, 4, 16, PTS), BF)
    for half in range(2):
        whole = ysend[half, mine[half][1]].astype(F32)
        for k in range(1, 4):
            whole = whole + ry[half, peers[half][1](k)].astype(F32)
        for part in range(5):
            zsend[part, 2 * half:2 * half + 2] = whole[2 * part:2 * part + 2].astype(BF)
        if half == 1:
            high, low = split(whole[8] + whole[9])
            zsend[4, 2] = jnp.where(odd, high.astype(F32), whole[8]).astype(BF)
            zsend[4, 3] = jnp.where(odd, low.astype(F32), whole[9]).astype(BF)
    for k in range(1, NZ):
        push(zsend.at[z_peer(k)], rz.at[z], 2, (sec, at(x, z_peer(k), y)))
    across(0)
    across(1)
    across(7)
    lax.fori_loop(12, 16, contact, 0, unroll=2)

    def balance(g, c, n):
        both = dot(stm[g], comps(g, c, n))
        for i in range(n):
            h = jnp.where(c + i <= HARM, c + i, c + i - HARM)
            scaled = jnp.asarray(h, jnp.int32).astype(F32) * freq[...]
            lanes = slice(i * PTS, (i + 1) * PTS)
            resid[g * NC + c + i] = both[0:ND, lanes] - (scaled * scaled) * both[ND:2 * ND, lanes]

    def balance_pair(g, i, carry):
        balance(g, 2 * i, 2)
        return carry

    arrived(rz.at[0:7], 2)
    whole = zsend[z].astype(F32)
    for k in range(1, NZ):
        whole = whole + rz[z_peer(k)].astype(F32)
    high, low = split(whole[2] + whole[3])
    here = jnp.logical_and(odd, z == 4)
    agz[z, 0:2] = whole[0:2].astype(BF)
    agz[z, 2] = jnp.where(here, high.astype(F32), whole[2]).astype(BF)
    agz[z, 3] = jnp.where(here, low.astype(F32), whole[3]).astype(BF)
    for k in range(1, NZ):
        push(agz.at[z], agz.at[z], 3, (sec, at(x, z_peer(k), y)))
    along(3)
    along(5)
    across(2)
    across(6)
    lax.fori_loop(0, 5, functools.partial(balance_pair, 0), 0)

    arrived(agz.at[0:7], 3)
    for half in range(2):
        agy[half, mine[half][1]] = agz[0:5, 2 * half:2 * half + 2].reshape(10, 16, PTS)
        for k in range(1, 4):
            slot = agy.at[half, mine[half][1]]
            push(slot, slot, 4, device(half, 1, k))
    lax.fori_loop(5, 9, functools.partial(balance_pair, 0), 0)
    balance(0, 18, 1)

    arrived(agy.at[:, 0:3], 4)
    for half in range(2):
        agx[half, mine[half][0]] = agy[half].reshape(2, 20, 16, PTS)
        for k in range(1, 4):
            slot = agx.at[half, mine[half][0]]
            push(slot, slot, 5, device(half, 0, k))
    lax.fori_loop(0, 9, functools.partial(balance_pair, 1), 0, unroll=3)
    balance(1, 18, 1)
    arrived(agx.at[:, 0:3], 5)

    lane128 = lax.broadcasted_iota(jnp.int32, (ROWS, ROWS), 1).astype(F32)
    eval_col = jnp.transpose(jnp.broadcast_to(eval_row, (ROWS, ROWS)))
    pre_col = jnp.transpose(jnp.broadcast_to(pre_row, (ROWS, ROWS)))
    choose = jnp.where(lane128 == eval_col, 1.0, 0.0).astype(BF)

    def joints(half, k):
        return agx[half, :, :, k].reshape(NDEV, PTS)

    loaded = dot(choose, jnp.concatenate([joints(1, 18), joints(1, 19)], axis=1))
    per_load = 1.0 / (loaded[:, 0:PTS] + loaded[:, PTS:2 * PTS])
    pressed = pre_col * (FRICTION * ROWS) * per_load

    def forces(half, c, carry):
        k = 2 * c - 20 * half
        mean = dot(choose, jnp.concatenate([joints(half, k), joints(half, k + 1)], axis=1))
        for a in range(2):
            rows = slice(a * ROWS, (a + 1) * ROWS)
            away = pay[c, rows, :] - mean[:, a * PTS:(a + 1) * PTS] * per_load
            force[c, rows, :] = (STIFF * away + pressed * harm[c, rows, :]).astype(BF)
        return carry

    lax.fori_loop(0, 10, functools.partial(forces, 0), 0, unroll=2)
    lax.fori_loop(10, NC, functools.partial(forces, 1), 0, unroll=3)

    across(4)

    def finish(g, c, n):
        lines = [force[c + i] for i in range(n)]
        added = dot(scat[g], lines[0] if n == 1 else jnp.concatenate(lines, axis=1))
        for i in range(n):
            item = g * NC + c + i
            value = resid[item] + added[:, i * PTS:(i + 1) * PTS]
            near[item] = value[0:NIF]
            far[item] = value[NIF:ND].astype(BF)

    def finish_pair(g, i, carry):
        finish(g, 2 * i, 2)
        return carry

    stores = []
    for g in range(2):
        lax.fori_loop(0, 9, functools.partial(finish_pair, g), 0, unroll=3)
        finish(g, 18, 1)
        block = pl.ds(g * NC, NC)
        stores.append(pltpu.make_async_copy(far.at[block], part_b.at[block], l_sem.at[5 + g]))
        stores.append(pltpu.make_async_copy(near.at[block], part_f.at[block], l_sem.at[7 + g]))
        stores[-2].start()
        stores[-1].start()
        if g == 0:
            across(3)

    across(5)
    left(rx.at[:, 0:3], 0)
    left(ry.at[:, 0:3], 1)
    left(rz.at[0:7], 2)
    left(agz.at[0:7], 3)
    left(agy.at[:, 0:3], 4)
    left(agx.at[:, 0:3], 5)
    for store in stores:
        store.wait()
    pltpu.make_async_copy(relay.at[0:7], relay.at[0:7], z_send).wait()
    pltpu.make_async_copy(relay_tags.at[0:7], relay_tags.at[0:7], zt_send).wait()
    pltpu.make_async_copy(packed, packed, s_send).wait()
    pltpu.make_async_copy(tags, tags, t_send).wait()
    pltpu.make_async_copy(got_tags, got_tags, t_recv).wait()
    pltpu.make_async_copy(got, got, s_recv).wait()


def last_kernel(
    got_h, tags_h, part_f, part_b, coupling, out_h,
    got, tags, near, out, glued, link, sems,
):
    tag_copy = pltpu.make_async_copy(tags_h, tags, sems.at[0])
    got_copy = pltpu.make_async_copy(got_h, got, sems.at[1])
    near_copy = pltpu.make_async_copy(part_f, near, sems.at[2])
    tag_copy.start()
    got_copy.start()
    near_copy.start()
    fars = []
    for g in range(2):
        block = pl.ds(g * NC, NC)
        fars.append(pltpu.make_async_copy(part_b.at[block], out.at[block, NIF:ND], sems.at[3 + g]))
        fars[g].start()
    glued[...] = jnp.zeros_like(glued)
    link[...] = jnp.zeros_like(link)
    for g in range(2):
        for q in range(4):
            span = slice(32 * q, 32 * q + 32)
            link[g, span, span] = jnp.transpose(coupling[g, q].astype(F32)).astype(BF)
    tag_copy.wait()
    got_copy.wait()

    def add(d, carry):
        for s in range(2):
            slot = tags[d, 0, 64 * s]
            glued[s, slot] = glued[s, slot] + got[d, 32 * s:32 * s + 32, :].astype(F32)
        return carry

    lax.fori_loop(0, NDEV, add, 0, unroll=4)
    near_copy.wait()

    def item(g, c):
        span = pl.ds((g * NC + c) * 4, 4)
        return (glued[0, span] + glued[1, span]).reshape(NIF, PTS).astype(BF)

    def finish(g, c, n):
        tiles = [item(g, c + i) for i in range(n)]
        added = dot(link[g], tiles[0] if n == 1 else jnp.concatenate(tiles, axis=1))
        for i in range(n):
            at = g * NC + c + i
            out[at, 0:NIF] = (near[at] + added[:, i * PTS:(i + 1) * PTS]).astype(BF)

    def finish_pair(g, i, carry):
        finish(g, 2 * i, 2)
        return carry

    stores = []
    for g in range(2):
        lax.fori_loop(0, 9, functools.partial(finish_pair, g), 0, unroll=3)
        finish(g, 18, 1)
        block = pl.ds(g * NC, NC)
        fars[g].wait()
        stores.append(pltpu.make_async_copy(out.at[block], out_h.at[block], sems.at[5 + g]))
        stores[g].start()
    for store in stores:
        store.wait()


def body(modal, stiffness, mass, freq, coupling, route, target, contact_dof, evaluator, preload):
    slope_table, proj_table = fourier_tables()
    vmem = pl.BlockSpec(memory_space=pltpu.VMEM)
    anywhere = pl.BlockSpec(memory_space=pl.ANY)
    dma = pltpu.SemaphoreType.DMA
    part_f, part_b, got, got_tags = pl.pallas_call(
        main_kernel,
        out_shape=(
            jax.ShapeDtypeStruct((2 * NC, NIF, PTS), F32),
            jax.ShapeDtypeStruct((2 * NC, ND - NIF, PTS), BF),
            jax.ShapeDtypeStruct((NDEV, 64, PTS), BF),
            jax.ShapeDtypeStruct((NDEV, 1, 128), jnp.int32),
        ),
        in_specs=[anywhere] * 3 + [vmem] * 8,
        out_specs=(anywhere,) * 4,
        scratch_shapes=[
            pltpu.VMEM((2 * NC, 4, 32, PTS), BF),
            pltpu.VMEM((2 * NC, 12, 32, PTS), BF),
            pltpu.VMEM((2, ND, ND), BF),
            pltpu.VMEM((2, ND, ND), BF),
            pltpu.VMEM((NDEV, 128), jnp.int32),
            pltpu.SMEM((NDEV, 128), jnp.int32),
            pltpu.VMEM((NDEV, 1, 128), jnp.int32),
            pltpu.VMEM((NDEV, 64, PTS), BF),
            pltpu.VMEM((2, 4, 2, 20, 16, PTS), BF),
            pltpu.VMEM((2, 4, 2, 20, 16, PTS), BF),
            pltpu.VMEM((2, 4, 10, 16, PTS), BF),
            pltpu.VMEM((2, 4, 10, 16, PTS), BF),
            pltpu.VMEM((NZ, 4, 16, PTS), BF),
            pltpu.VMEM((NZ, 4, 16, PTS), BF),
            pltpu.VMEM((NZ, 4, 16, PTS), BF),
            pltpu.VMEM((2, 4, 10, 16, PTS), BF),
            pltpu.VMEM((2, 4, 2, 20, 16, PTS), BF),
            pltpu.VMEM((NC, 2 * ROWS, PTS), F32),
            pltpu.VMEM((NC, 2 * ROWS, PTS), F32),
            pltpu.VMEM((NC, 2 * ROWS, PTS), BF),
            pltpu.VMEM((2 * NC, ND, PTS), F32),
            pltpu.VMEM((2, 2 * ND, ND), BF),
            pltpu.VMEM((2, ND, 2 * ROWS), BF),
            pltpu.VMEM((2 * NC, NIF, PTS), F32),
            pltpu.VMEM((2 * NC, ND - NIF, PTS), BF),
            pltpu.VMEM((NZ, 16, 64, PTS), BF),
            pltpu.VMEM((NZ, 16, 1, 128), jnp.int32),
            dma((9,)), dma, dma, dma, dma, dma((6,)), dma((6,)), dma, dma((NZ,)), dma, dma((NZ,)),
        ],
        compiler_params=pltpu.CompilerParams(
            collective_id=1, has_side_effects=True, vmem_limit_bytes=58 << 20
        ),
    )(modal.reshape(2 * NC, 16, 32, PTS), stiffness[0], mass[0], freq.reshape(1, PTS),
      preload, evaluator.reshape(1, ROWS), contact_dof, route.reshape(1, TILES), target,
      jnp.asarray(slope_table), jnp.asarray(proj_table))

    out = pl.pallas_call(
        last_kernel,
        out_shape=jax.ShapeDtypeStruct((2 * NC, ND, PTS), BF),
        in_specs=[anywhere] * 4 + [vmem],
        out_specs=anywhere,
        scratch_shapes=[
            pltpu.VMEM((NDEV, 64, PTS), BF),
            pltpu.SMEM((NDEV, 1, 128), jnp.int32),
            pltpu.VMEM((2 * NC, NIF, PTS), F32),
            pltpu.VMEM((2 * NC, ND, PTS), BF),
            pltpu.VMEM((2, TILES + 1, 32, PTS), F32),
            pltpu.VMEM((2, NIF, NIF), BF),
            dma((7,)),
        ],
        compiler_params=pltpu.CompilerParams(vmem_limit_bytes=58 << 20),
    )(got, got_tags, part_f, part_b, coupling[0])
    return out.reshape(1, 2, NC, ND, PTS)


def solution(mesh):
    placed = (
        P("section", "diam", None, None, None),
        P("section", "diam", None, None),
        P("section", "diam", None, None),
        P(),
        P("section", "diam", None, None, None),
        P("section", "diam", None),
        P("section", "diam"),
        P("section", "diam"),
        P("section", "diam", None),
        P("section", "diam"),
    )
    return jax.shard_map(
        body,
        mesh=mesh,
        in_specs=placed,
        out_specs=P("section", "diam", None, None, None),
        check_vma=False,
    )
```
